256 devices in a mesh: units: 256 (over y, x, z, core).
Axes of the slice: x: 4, y: 4, z: 8, core: 2. Of those that a mesh axis runs over, the one named last changes fastest.
Arguments:
- unit_data: bfloat16 [524288, 384], P('units'), may hold values from -6 to 6
- owner: int32 [1], replicated, may hold values from 0 to 255
Outputs:
- owner_grad: float32 [2048, 256], replicated
- local_grad: float32 [524288, 256], P('units')
The draws below stay inside these ranges and needn't reach their ends.
All inputs are finite; a program needn't handle non-finite values.
Results may differ from the reference program's by a relative error of at most 0.0022.
Values may be sent and summed in bfloat16 or wider, within the bound.
No kernel may reach another device: no remote copies, remote signals or barrier semaphores. Data moves between devices by JAX's collectives and lax.ppermute only.
A program may use at most 64 MiB of HBM per device.

```python
import math
import jax
import jax.numpy as jnp
from jax import lax

D = 256
COLS = 64
ROWS_DEV = 2048
UNITS = 524288
N_UNITS = 256


def steps_of(stream_key, extent, cuts, smallest, high):
    gain = 1.0
    for dim, parts in cuts:
        steps = jax.random.uniform(jax.random.fold_in(jax.random.fold_in(stream_key, 6), dim), (parts,), jnp.float32, smallest / len(cuts), high / len(cuts))
        gain = gain * jnp.repeat(jnp.exp(steps), extent[dim] // parts).reshape((-1,) + (1,) * (len(extent) - 1 - dim))
    return gain


def scatter_about(own_key, dims, deviation, bound, split=(), kind=jnp.bfloat16):
    entries = deviation * jax.random.normal(own_key, dims, jnp.float32)
    if split:
        entries = entries * steps_of(own_key, dims, split, -0.22, 0.18)
    return jnp.clip(entries, -bound, bound).astype(kind)


def setup_inputs(seed: int = 0) -> dict:
    seeds = jax.random.split(jax.random.key(seed), 3)
    unit_data = scatter_about(seeds[0], (UNITS, D + 2 * COLS), 1.0, 6.0, ((0, 256),))
    owner = jax.random.randint(seeds[1], (1,), 0, N_UNITS).astype(jnp.int32)
    return dict(unit_data=unit_data, owner=owner)


def pair_terms(owner_block, unit_block):
    owner_feat = owner_block[:, :D]
    owner_sol = owner_block[:, D:D + COLS]
    owner_probe = owner_block[:, D + COLS:]
    unit_feat = unit_block[:, :D]
    unit_sol = unit_block[:, D:D + COLS]
    unit_probe = unit_block[:, D + COLS:]
    owner_wide = owner_feat.astype(jnp.float32)
    unit_wide = unit_feat.astype(jnp.float32)
    owner_sq = lax.optimization_barrier(jnp.sum(owner_wide * owner_wide, axis=1))
    unit_sq = lax.optimization_barrier(jnp.sum(unit_wide * unit_wide, axis=1))
    cross = jnp.dot(owner_feat, unit_feat.T, preferred_element_type=jnp.float32)
    kernel = jnp.exp(-(owner_sq[:, None] + unit_sq[None, :] - 2.0 * cross) / (2.0 * D))
    weight = jnp.dot(owner_sol, unit_probe.T, preferred_element_type=jnp.float32)
    weight = weight + jnp.dot(owner_probe, unit_sol.T, preferred_element_type=jnp.float32)
    weight = weight * (0.5 / math.sqrt(COLS))
    mixed = weight * kernel
    mixed_b = mixed.astype(jnp.bfloat16)
    owner_term = jnp.dot(mixed_b, unit_feat, preferred_element_type=jnp.float32) - lax.optimization_barrier(jnp.sum(mixed, axis=1))[:, None] * owner_wide
    local_term = jnp.dot(mixed_b.T, owner_feat, preferred_element_type=jnp.float32) - lax.optimization_barrier(jnp.sum(mixed, axis=0))[:, None] * unit_wide
    return (owner_term, local_term)

def reference(unit_data, owner):
    row_start = (owner[0] * ROWS_DEV).astype(jnp.int32)
    owner_block = lax.dynamic_slice_in_dim(unit_data, row_start, ROWS_DEV, 0)
    blocks = unit_data.reshape(N_UNITS, ROWS_DEV, D + 2 * COLS)

    def visit(carry, unit_block):
        owner_term, local_term = pair_terms(owner_block, unit_block)
        return (carry + owner_term, local_term)
    total, locals_all = lax.scan(visit, jnp.zeros((ROWS_DEV, D), jnp.float32), blocks)
    owner_grad = total * (1.0 / math.sqrt(UNITS))
    local_grad = locals_all.reshape(UNITS, D) * (1.0 / math.sqrt(ROWS_DEV))
    return (owner_grad, local_grad)
```

```python
import math

import jax
import jax.numpy as jnp
import numpy as np
from jax import lax
from jax.sharding import Mesh
from jax.sharding import PartitionSpec as P

D = 256
COLS = 64
PLANE = ("y", "x")
ALL = ("y", "x", "z", "c")
NY, NX, NZ, NC = 4, 4, 8, 2


def swap(v):
    return lax.ppermute(v, "c", [(0, 1), (1, 0)])


def exchange(v, axis):
    return lax.all_to_all(v, axis, 0, 0, tiled=True)


def pick(v, parts, index):
    rows = v.shape[0] // parts
    return lax.dynamic_slice_in_dim(v, index * rows, rows, 0)


def repeat(v, parts):
    return jnp.broadcast_to(v[None], (parts, *v.shape)).reshape(parts * v.shape[0], *v.shape[1:])


def broadcast_half(mine, theirs, owner):
    oc = owner % NC
    oz = owner // NC % NZ
    plane = owner // (NC * NZ)
    half = jnp.where(oc == lax.axis_index("c"), mine, theirs)
    piece = pick(exchange(half, PLANE), NY * NX, plane)
    piece = pick(exchange(repeat(piece, NZ), "z"), NZ, oz)
    return exchange(repeat(piece, NY * NX), PLANE)


def reduce_half(term):
    rows = term.shape[0] // (NY * NX)
    piece = jnp.sum(exchange(term, PLANE).reshape(NY * NX, rows, D), axis=0)
    piece = jnp.sum(exchange(repeat(piece, NZ), "z").reshape(NZ, rows, D), axis=0)
    return exchange(repeat(piece, NY * NX), PLANE)


def pair_terms(owner_block, unit_block):
    owner_feat = owner_block[:, :D]
    unit_feat = unit_block[:, :D]
    owner_wide = owner_feat.astype(jnp.float32)
    unit_wide = unit_feat.astype(jnp.float32)
    owner_sq = jnp.sum(owner_wide * owner_wide, axis=1)
    unit_sq = jnp.sum(unit_wide * unit_wide, axis=1)
    contract_last = (((1,), (1,)), ((), ()))
    cross = lax.dot_general(owner_feat, unit_feat, contract_last, preferred_element_type=jnp.float32)
    kernel = jnp.exp(-(owner_sq[:, None] + unit_sq[None, :] - 2.0 * cross) / (2.0 * D))
    swapped = jnp.concatenate([unit_block[:, D + COLS :], unit_block[:, D : D + COLS]], axis=1)
    weight = lax.dot_general(owner_block[:, D:], swapped, contract_last, preferred_element_type=jnp.float32)
    mixed = weight * (0.5 / math.sqrt(COLS)) * kernel
    mixed_b = mixed.astype(jnp.bfloat16)
    owner_term = (
        jnp.dot(mixed_b, unit_feat, preferred_element_type=jnp.float32)
        - jnp.sum(mixed, axis=1)[:, None] * owner_wide
    )
    contract_first = (((0,), (0,)), ((), ()))
    local_term = (
        lax.dot_general(mixed_b, owner_feat, contract_first, preferred_element_type=jnp.float32)
        - jnp.sum(mixed, axis=0)[:, None] * unit_wide
    )
    return (owner_term, local_term)


def local(unit_data, owner):
    rows = unit_data.shape[0]
    half_rows = rows // NC
    core = lax.axis_index("c")
    here = pick(unit_data, NC, core)
    there = pick(unit_data, NC, 1 - core)
    here_other = swap(there)
    there_other = swap(here)
    owner_half = broadcast_half(here, here_other, owner[0])
    both = jnp.concatenate([here, there, here_other, there_other], axis=0)
    owner_term, local_term = pair_terms(owner_half, both)
    summed = reduce_half(owner_term) * (1.0 / math.sqrt(rows * NY * NX * NZ * NC))
    summed_other = swap(summed)
    owner_grad = jnp.concatenate(
        [jnp.where(core == 0, summed, summed_other), jnp.where(core == 0, summed_other, summed)], axis=0
    )
    received = swap(local_term[rows:])
    local_sum = (local_term[:rows] + jnp.concatenate([received[half_rows:], received[:half_rows]], axis=0)) * (
        1.0 / math.sqrt(rows)
    )
    first = local_sum[:half_rows]
    second = local_sum[half_rows:]
    local_grad = jnp.concatenate(
        [jnp.where(core == 0, first, second), jnp.where(core == 0, second, first)], axis=0
    )
    return (owner_grad, local_grad)


def solution(mesh):
    grid = Mesh(np.asarray(mesh.devices).reshape(NY, NX, NZ, NC), ALL)
    in_specs = (P(ALL, None), P())
    out_specs = (P(), P(ALL, None))
    return jax.shard_map(local, mesh=grid, in_specs=in_specs, out_specs=out_specs, check_vma=False)
```

```python
import functools
import math

import jax
import jax.numpy as jnp
import numpy as np
from jax import lax
from jax.experimental import pallas as pl
from jax.experimental.pallas import tpu as pltpu
from jax.sharding import Mesh
from jax.sharding import PartitionSpec as P

D = 256
COLS = 64
WIDE = D + 2 * COLS
PLANE = ("y", "x")
ALL = ("y", "x", "z", "c")
NY, NX, NZ, NC = 4, 4, 8, 2
NP = NY * NX
LOG2E = math.log2(math.e)
TILE_UNITS = 1024
TILE_OWNER = 256
SCALE_ROWS = 16


def swap(v):
    return lax.ppermute(v, "c", [(0, 1), (1, 0)])


def shift(v, k):
    return lax.ppermute(v, "z", [(i, (i + k) % NZ) for i in range(NZ)])


def exchange(v):
    return lax.all_to_all(v, PLANE, 0, 0, tiled=True)


def pick(v, parts, index):
    rows = v.shape[0] // parts
    return lax.dynamic_slice_in_dim(v, index * rows, rows, 0)


def repeat(v):
    return jnp.broadcast_to(v[None], (NP, *v.shape))


def along_z(v, root):
    away = (lax.axis_index("z") - root) % NZ
    v = jnp.where(away == 4, shift(v, 4), v)
    up, down, two = shift(v, 1), shift(v, -1), shift(v, 2)
    step = away % 4
    return jnp.where(step == 0, v, jnp.where(step == 1, up, jnp.where(step == 3, down, two)))


def sum_z(v):
    v = v + shift(v, 4)
    return (v + shift(v, 2)) + (shift(v, 1) + shift(v, -1))


def broadcast_half(block, owner):
    core = lax.axis_index("c")
    other = swap(pick(block, NC, 1 - core))
    half = jnp.where(owner % NC == core, pick(block, NC, core), other)
    piece = pick(exchange(half), NP, owner // (NC * NZ))
    piece = along_z(piece, owner // NC % NZ)
    return exchange(repeat(piece)).reshape(half.shape)


def pack(v):
    top = jnp.max(jnp.abs(v), axis=(-2, -1), keepdims=True)
    power = jnp.floor(jnp.log2(jnp.maximum(top, 1e-30))) - 13.0
    scaled = (v * jnp.exp2(-power)).astype(jnp.float16)
    extra = jnp.broadcast_to(power, (*v.shape[:-2], SCALE_ROWS, v.shape[-1])).astype(jnp.float16)
    return jnp.concatenate([scaled, extra], axis=-2)


def unpack(v, factor=1.0):
    scale = jnp.exp2(v[..., -SCALE_ROWS : 1 - SCALE_ROWS, :1].astype(jnp.float32)) * factor
    return v[..., :-SCALE_ROWS, :].astype(jnp.float32) * scale


def reduce_half(term, factor):
    rows = term.shape[0] // NP
    piece = jnp.sum(unpack(exchange(pack(term.reshape(NP, rows, D)))), axis=0)
    piece = sum_z(piece)
    mine = exchange(repeat(pack(piece)))
    other = swap(mine)
    first = lax.axis_index("c") == 0
    mine = unpack(mine, factor).reshape(term.shape)
    other = unpack(other, factor).reshape(term.shape)
    return jnp.concatenate([jnp.where(first, mine, other), jnp.where(first, other, mine)], axis=0)


def mix_kernel(own_ref, unit_ref, sq_ref, mix_ref, term_ref, col_ref, own_sq, row_sum, *, steps):
    j = pl.program_id(0)
    rows = own_ref.shape[0]
    spans = [slice(i, i + TILE_OWNER) for i in range(0, rows, TILE_OWNER)]

    @pl.when(j == 0)
    def _():
        term_ref[...] = jnp.zeros_like(term_ref)
        row_sum[...] = jnp.zeros_like(row_sum)
        for span in spans:
            feat = own_ref[span, :D].astype(jnp.float32)
            own_sq[span, :] = jnp.sum(feat * feat, axis=1, keepdims=True) * (LOG2E / (2.0 * D)) + math.log2(
                2.0 * math.sqrt(COLS)
            )

    feat = unit_ref[:, :D]
    swapped = jnp.concatenate([unit_ref[:, D + COLS :], unit_ref[:, D : D + COLS]], axis=1)
    col = jnp.zeros(col_ref.shape, jnp.float32)
    contract_last = (((1,), (1,)), ((), ()))
    for span in spans:
        cross = lax.dot_general(own_ref[span, :D], feat, contract_last, preferred_element_type=jnp.float32)
        weight = lax.dot_general(own_ref[span, D:], swapped, contract_last, preferred_element_type=jnp.float32)
        mixed = weight * jnp.exp2(cross * (LOG2E / D) - sq_ref[...] - own_sq[span, :])
        mixed_b = mixed.astype(jnp.bfloat16)
        mix_ref[span, :] = mixed_b
        term_ref[span, :] += jnp.dot(mixed_b, feat, preferred_element_type=jnp.float32)
        col = col + jnp.sum(mixed.reshape(-1, *col.shape), axis=0)
        lanes = mixed[:, :128]
        for start in range(128, mixed.shape[1], 128):
            lanes = lanes + mixed[:, start : start + 128]
        row_sum[span, :] += lanes
    col_ref[...] = col

    @pl.when(j == steps - 1)
    def _():
        for span in spans:
            total = jnp.sum(row_sum[span, :], axis=1, keepdims=True)
            term_ref[span, :] -= total * own_ref[span, :D].astype(jnp.float32)


def mix(own, units, unit_sq):
    rows, count = own.shape[0], units.shape[0]
    steps = count // TILE_UNITS
    return pl.pallas_call(
        functools.partial(mix_kernel, steps=steps),
        grid=(steps,),
        in_specs=[
            pl.BlockSpec((rows, WIDE), lambda j: (0, 0)),
            pl.BlockSpec((TILE_UNITS, WIDE), lambda j: (j, 0)),
            pl.BlockSpec((1, TILE_UNITS), lambda j: (0, j)),
        ],
        out_specs=[
            pl.BlockSpec((rows, TILE_UNITS), lambda j: (0, j)),
            pl.BlockSpec((rows, D), lambda j: (0, 0)),
            pl.BlockSpec((8, TILE_UNITS), lambda j: (0, j)),
        ],
        out_shape=[
            jax.ShapeDtypeStruct((rows, count), jnp.bfloat16),
            jax.ShapeDtypeStruct((rows, D), jnp.float32),
            jax.ShapeDtypeStruct((8, count), jnp.float32),
        ],
        scratch_shapes=[pltpu.VMEM((rows, 1), jnp.float32), pltpu.VMEM((rows, 128), jnp.float32)],
        compiler_params=pltpu.CompilerParams(
            vmem_limit_bytes=24 * 2**20, dimension_semantics=("arbitrary",)
        ),
        cost_estimate=pl.CostEstimate(
            flops=2 * rows * count * (WIDE + D),
            bytes_accessed=2 * rows * count + 2 * WIDE * (rows + count) + 4 * rows * D,
            transcendentals=rows * count,
        ),
    )(own, units, unit_sq)


def local(unit_data, owner):
    rows = unit_data.shape[0]
    owner_half = broadcast_half(unit_data, owner[0])
    both = jnp.concatenate([unit_data, swap(unit_data)], axis=0)
    both_wide = both[:, :D].astype(jnp.float32)
    unit_sq = jnp.sum(both_wide * both_wide, axis=1) * (LOG2E / (2.0 * D))
    mixed_b, owner_term, col_parts = mix(owner_half, both, unit_sq[None, :])
    owner_grad = reduce_half(owner_term, 1.0 / math.sqrt(rows * NP * NZ * NC))
    contract_first = (((0,), (0,)), ((), ()))
    local_term = (
        lax.dot_general(mixed_b, owner_half[:, :D], contract_first, preferred_element_type=jnp.float32)
        - jnp.sum(col_parts, axis=0)[:, None] * both_wide
    )
    local_grad = (local_term[:rows] + swap(local_term[rows:])) * (1.0 / math.sqrt(rows))
    return (owner_grad, local_grad)


def solution(mesh):
    grid = Mesh(np.asarray(mesh.devices).reshape(NY, NX, NZ, NC), ALL)
    in_specs = (P(ALL, None), P())
    out_specs = (P(), P(ALL, None))
    return jax.shard_map(local, mesh=grid, in_specs=in_specs, out_specs=out_specs, check_vma=False)
```

```python
import functools
import math

import jax
import jax.numpy as jnp
import numpy as np
from jax import lax
from jax.experimental import pallas as pl
from jax.experimental.pallas import tpu as pltpu
from jax.sharding import Mesh
from jax.sharding import PartitionSpec as P

D = 256
COLS = 64
WIDE = D + 2 * COLS
PLANE = ("y", "x")
ALL = ("y", "x", "z", "c")
NY, NX, NZ, NC = 4, 4, 8, 2
NP = NY * NX
LOG2E = math.log2(math.e)
TILE_UNITS = 1024
TILE_OWNER = 256
SCALE_ROWS = 16


def swap(v):
    return lax.ppermute(v, "c", [(0, 1), (1, 0)])


def shift(v, k):
    return lax.ppermute(v, "z", [(i, (i + k) % NZ) for i in range(NZ)])


def exchange(v):
    return lax.all_to_all(v, PLANE, 0, 0, tiled=True)


def pick(v, parts, index):
    rows = v.shape[0] // parts
    return lax.dynamic_slice_in_dim(v, index * rows, rows, 0)


def repeat(v):
    return jnp.broadcast_to(v[None], (NP, *v.shape))


def along_z(v, root):
    away = (lax.axis_index("z") - root) % NZ
    v = jnp.where(away == 4, shift(v, 4), v)
    up, down, two = shift(v, 1), shift(v, -1), shift(v, 2)
    step = away % 4
    return jnp.where(step == 0, v, jnp.where(step == 1, up, jnp.where(step == 3, down, two)))


def sum_z(v):
    v = v + shift(v, 4)
    return (v + shift(v, 2)) + (shift(v, 1) + shift(v, -1))


def tie(*values):
    return lax.optimization_barrier(values)


def broadcast_half(block, owner):
    core = lax.axis_index("c")
    there = pick(block, NC, 1 - core)
    here = pick(block, NC, core)
    other = swap(there)
    here, other = tie(here, other)
    half = jnp.where(owner % NC == core, here, other)
    piece = pick(exchange(half), NP, owner // (NC * NZ))
    piece, block = tie(piece, block)
    partner = swap(block)
    squares = jnp.concatenate([squared(block), squared(partner)])[None, :]
    piece = along_z(piece, owner // NC % NZ)
    piece, partner, squares = tie(piece, partner, squares)
    return exchange(repeat(piece)).reshape(half.shape), partner, squares


def squared(block):
    wide = block[:, :D].astype(jnp.float32)
    return jnp.sum(wide * wide, axis=1) * (LOG2E / (2.0 * D))


def pack(v):
    top = jnp.max(jnp.abs(v), axis=(-2, -1), keepdims=True)
    power = jnp.floor(jnp.log2(jnp.maximum(top, 1e-30))) - 13.0
    scaled = (v * jnp.exp2(-power)).astype(jnp.float16)
    extra = jnp.broadcast_to(power, (*v.shape[:-2], SCALE_ROWS, v.shape[-1])).astype(jnp.float16)
    return jnp.concatenate([scaled, extra], axis=-2)


def unpack(v, factor=1.0):
    scale = jnp.exp2(v[..., -SCALE_ROWS : 1 - SCALE_ROWS, :1].astype(jnp.float32)) * factor
    return v[..., :-SCALE_ROWS, :].astype(jnp.float32) * scale


def mix_kernel(own_ref, unit_ref, partner_ref, sq_ref, mix_ref, term_ref, col_ref, own_sq, row_sum, *, steps):
    j = pl.program_id(0)
    rows = own_ref.shape[0]
    spans = [slice(i, i + TILE_OWNER) for i in range(0, rows, TILE_OWNER)]

    @pl.when(j == 0)
    def _():
        term_ref[...] = jnp.zeros_like(term_ref)
        row_sum[...] = jnp.zeros_like(row_sum)
        for span in spans:
            feat = own_ref[span, :D].astype(jnp.float32)
            own_sq[span, :] = jnp.sum(feat * feat, axis=1, keepdims=True) * (LOG2E / (2.0 * D)) + math.log2(
                2.0 * math.sqrt(COLS)
            )

    units = jnp.where(j < steps // 2, unit_ref[...], partner_ref[...])
    feat = units[:, :D]
    swapped = jnp.concatenate([units[:, D + COLS :], units[:, D : D + COLS]], axis=1)
    col = jnp.zeros(col_ref.shape, jnp.float32)
    contract_last = (((1,), (1,)), ((), ()))
    for span in spans:
        cross = lax.dot_general(own_ref[span, :D], feat, contract_last, preferred_element_type=jnp.float32)
        weight = lax.dot_general(own_ref[span, D:], swapped, contract_last, preferred_element_type=jnp.float32)
        mixed = weight * jnp.exp2(cross * (LOG2E / D) - sq_ref[...] - own_sq[span, :])
        mixed_b = mixed.astype(jnp.bfloat16)
        mix_ref[span, :] = mixed_b
        term_ref[span, :] += jnp.dot(mixed_b, feat, preferred_element_type=jnp.float32)
        col = col + jnp.sum(mixed.reshape(-1, *col.shape), axis=0)
        lanes = mixed[:, :128]
        for start in range(128, mixed.shape[1], 128):
            lanes = lanes + mixed[:, start : start + 128]
        row_sum[span, :] += lanes
    col_ref[...] = col

    @pl.when(j == steps - 1)
    def _():
        for span in spans:
            total = jnp.sum(row_sum[span, :], axis=1, keepdims=True)
            term_ref[span, :] -= total * own_ref[span, :D].astype(jnp.float32)


def mix(own, units, partner, unit_sq):
    rows, count = own.shape[0], units.shape[0] + partner.shape[0]
    steps = count // TILE_UNITS
    half = steps // 2
    return pl.pallas_call(
        functools.partial(mix_kernel, steps=steps),
        grid=(steps,),
        in_specs=[
            pl.BlockSpec((rows, WIDE), lambda j: (0, 0)),
            pl.BlockSpec((TILE_UNITS, WIDE), lambda j: (jnp.minimum(j, half - 1), 0)),
            pl.BlockSpec((TILE_UNITS, WIDE), lambda j: (jnp.maximum(j - half, 0), 0)),
            pl.BlockSpec((1, TILE_UNITS), lambda j: (0, j)),
        ],
        out_specs=[
            pl.BlockSpec((rows, TILE_UNITS), lambda j: (0, j)),
            pl.BlockSpec((rows, D), lambda j: (0, 0)),
            pl.BlockSpec((8, TILE_UNITS), lambda j: (0, j)),
        ],
        out_shape=[
            pltpu.HBM((rows, count), jnp.bfloat16),
            jax.ShapeDtypeStruct((rows, D), jnp.float32),
            jax.ShapeDtypeStruct((8, count), jnp.float32),
        ],
        scratch_shapes=[pltpu.VMEM((rows, 1), jnp.float32), pltpu.VMEM((rows, 128), jnp.float32)],
        compiler_params=pltpu.CompilerParams(
            vmem_limit_bytes=24 * 2**20, dimension_semantics=("arbitrary",)
        ),
        cost_estimate=pl.CostEstimate(
            flops=2 * rows * count * (WIDE + D),
            bytes_accessed=2 * rows * count + 2 * WIDE * (rows + count) + 4 * rows * D,
            transcendentals=rows * count,
        ),
    )(own, units, partner, unit_sq)


def local_kernel(mix_ref, own_ref, unit_ref, col_ref, *rest, scale):
    contract_first = (((0,), (0,)), ((), ()))
    out = lax.dot_general(mix_ref[...], own_ref[:, :D], contract_first, preferred_element_type=jnp.float32)
    total = jnp.sum(col_ref[...].T, axis=1, keepdims=True)
    out = out - total * unit_ref[:, :D].astype(jnp.float32)
    if len(rest) == 2:
        out = (out + rest[0][...]) * scale
    rest[-1][...] = out


def local_terms(mixed, own, units, col, first, received=None, scale=1.0):
    rows, count = own.shape[0], units.shape[0]
    base = first // TILE_UNITS
    specs = [
        pl.BlockSpec((rows, TILE_UNITS), lambda j: (0, j + base)),
        pl.BlockSpec((rows, WIDE), lambda j: (0, 0)),
        pl.BlockSpec((TILE_UNITS, WIDE), lambda j: (j, 0)),
        pl.BlockSpec((8, TILE_UNITS), lambda j: (0, j + base)),
    ]
    args = [pltpu.with_memory_space_constraint(mixed, pltpu.HBM), own, units, col]
    if received is not None:
        specs.append(pl.BlockSpec((TILE_UNITS, D), lambda j: (j, 0)))
        args.append(received)
    return pl.pallas_call(
        functools.partial(local_kernel, scale=scale),
        grid=(count // TILE_UNITS,),
        in_specs=specs,
        out_specs=pl.BlockSpec((TILE_UNITS, D), lambda j: (j, 0)),
        out_shape=jax.ShapeDtypeStruct((count, D), jnp.float32),
        compiler_params=pltpu.CompilerParams(
            vmem_limit_bytes=24 * 2**20, dimension_semantics=("arbitrary",)
        ),
        cost_estimate=pl.CostEstimate(
            flops=2 * rows * count * D, bytes_accessed=2 * rows * count + 8 * count * D, transcendentals=0
        ),
    )(*args)


def local(unit_data, owner):
    rows = unit_data.shape[0]
    own, partner, squares = broadcast_half(unit_data, owner[0])
    half_rows = own.shape[0]
    piece_rows = half_rows // NP
    mixed, term, col = mix(own, unit_data, partner, squares)
    pieces = exchange(pack(term.reshape(NP, piece_rows, D)))
    away = local_terms(mixed, own, partner, col, rows)
    pieces, away = tie(pieces, away)
    received = swap(away)
    piece = sum_z(jnp.sum(unpack(pieces), axis=0))
    piece, received = tie(piece, received)
    mine = exchange(repeat(pack(piece)))
    local_grad = local_terms(mixed, own, unit_data, col, 0, received, 1.0 / math.sqrt(rows))
    mine, local_grad = tie(mine, local_grad)
    other = swap(mine)
    factor = 1.0 / math.sqrt(rows * NP * NZ * NC)
    first = lax.axis_index("c") == 0
    mine = unpack(mine, factor).reshape(half_rows, D)
    other = unpack(other, factor).reshape(half_rows, D)
    owner_grad = jnp.concatenate([jnp.where(first, mine, other), jnp.where(first, other, mine)], axis=0)
    return (owner_grad, local_grad)


def solution(mesh):
    grid = Mesh(np.asarray(mesh.devices).reshape(NY, NX, NZ, NC), ALL)
    in_specs = (P(ALL, None), P())
    out_specs = (P(), P(ALL, None))
    return jax.shard_map(local, mesh=grid, in_specs=in_specs, out_specs=out_specs, check_vma=False)
```

```python
import functools
import math

import jax
import jax.numpy as jnp
import numpy as np
from jax import lax
from jax.experimental import pallas as pl
from jax.experimental.pallas import tpu as pltpu
from jax.sharding import Mesh
from jax.sharding import PartitionSpec as P

D = 256
COLS = 64
WIDE = D + 2 * COLS
PLANE = ("y", "x", "v")
ALL = ("y", "x", "w", "v", "c")
NY, NX, NW, NV, NC = 4, 4, 4, 2, 2
NP = NY * NX * NV
TILE_UNITS = 1024
TILE_OWNER = 256
SCALE_ROWS = 8
SMALL = 4 * 2**20


def swap(v):
    return lax.ppermute(v, "c", [(0, 1), (1, 0)])


def shift(v, k):
    return lax.ppermute(v, "w", [(i, (i + k) % NW) for i in range(NW)])


def exchange(v):
    return lax.all_to_all(v, PLANE, 0, 0, tiled=True)


def pick(v, parts, index):
    rows = v.shape[0] // parts
    return lax.dynamic_slice_in_dim(v, index * rows, rows, 0)


def repeat(v):
    return jnp.broadcast_to(v[None], (NP, *v.shape))


def along_w(v, root):
    away = (lax.axis_index("w") - root) % NW
    up, down, two = shift(v, 1), shift(v, -1), shift(v, 2)
    return jnp.where(away == 0, v, jnp.where(away == 1, up, jnp.where(away == 3, down, two)))


def all_w(v):
    return v, shift(v, 2), shift(v, 1), shift(v, -1)


def in_hbm(v):
    return pltpu.with_memory_space_constraint(v, pltpu.HBM)


def tie(*values):
    return lax.optimization_barrier(values)


def split_kernel(block_ref, here_ref, there_ref, sems):
    rows = here_ref.shape[0]
    core = lax.axis_index("c")
    copies = [
        pltpu.make_async_copy(
            block_ref.at[pl.ds(pl.multiple_of(index * rows, rows), rows)], target, sems.at[slot]
        )
        for slot, (index, target) in enumerate(((1 - core, there_ref), (core, here_ref)))
    ]
    for copy in copies:
        copy.start()
    for copy in copies:
        copy.wait()


def split(block):
    half = jax.ShapeDtypeStruct((block.shape[0] // NC, block.shape[1]), block.dtype)
    return pl.pallas_call(
        split_kernel,
        in_specs=[pl.BlockSpec(memory_space=pl.ANY)],
        out_specs=[pl.BlockSpec(memory_space=pltpu.VMEM)] * 2,
        out_shape=[half, half],
        scratch_shapes=[pltpu.SemaphoreType.DMA((2,))],
        compiler_params=pltpu.CompilerParams(vmem_limit_bytes=SMALL),
    )(in_hbm(block))


def broadcast_half(block, owner):
    here, there = split(block)
    level = owner // NC % (NW * NV)
    place = owner // (NC * NW * NV) * NV + level % NV
    here, other, level, place = tie(here, swap(there), level, place)
    half = jnp.where(owner % NC == lax.axis_index("c"), here, other)
    piece = pick(exchange(half), NP, place)
    piece, block = tie(piece, block)
    partner = swap(block)
    squares = jnp.concatenate([squared(block), squared(partner)])[None, :]
    piece = along_w(piece, level // NV)
    piece, partner, squares = tie(piece, partner, squares)
    return exchange(repeat(piece)).reshape(half.shape), partner, squares


def squared(block):
    wide = block[:, :D].astype(jnp.float32)
    return jnp.sum(wide * wide, axis=1) * (0.5 / D)


def scaled(v):
    top = jnp.max(jnp.abs(v), axis=(0, 1), keepdims=True)
    power = jnp.floor(jnp.log2(jnp.maximum(top, 1e-30))) - 13.0
    return jnp.concatenate([v * jnp.exp(power * -math.log(2.0)), jnp.broadcast_to(power, (SCALE_ROWS, D))], axis=0)


def unpack(v, factor=1.0):
    groups = v.reshape(v.shape[0], -1, SCALE_ROWS, D).astype(jnp.float32)
    wide = groups[:, :-1] * (jnp.exp2(groups[:, -1:]) * factor)
    return wide.reshape(v.shape[0], -1, D)


def join_kernel(*refs):
    refs[-1][...] = scaled((refs[0][...] + refs[1][...]) + (refs[2][...] + refs[3][...]))


def join(*parts):
    rows = parts[0].shape[0]
    return pl.pallas_call(
        join_kernel,
        out_shape=jax.ShapeDtypeStruct((rows + SCALE_ROWS, D), jnp.float32),
        compiler_params=pltpu.CompilerParams(vmem_limit_bytes=SMALL),
    )(*parts)


def mix_kernel(own_ref, unit_ref, partner_ref, sq_ref, mix_ref, term_ref, col_ref, total, own_sq, row_sum, *, steps):
    j = pl.program_id(0)
    rows = own_ref.shape[0]
    spans = [slice(i, i + TILE_OWNER) for i in range(0, rows, TILE_OWNER)]

    @pl.when(j == 0)
    def _():
        total[...] = jnp.zeros_like(total)
        row_sum[...] = jnp.zeros_like(row_sum)
        for span in spans:
            feat = own_ref[span, :D].astype(jnp.float32)
            own_sq[span, :] = jnp.sum(feat * feat, axis=1, keepdims=True) * (0.5 / D) + math.log(2.0 * math.sqrt(COLS))

    units = jnp.where(j < steps // 2, unit_ref[...], partner_ref[...])
    feat = units[:, :D]
    swapped = jnp.concatenate([units[:, D + COLS :], units[:, D : D + COLS]], axis=1)
    col = jnp.zeros(col_ref.shape, jnp.float32)
    contract_last = (((1,), (1,)), ((), ()))
    for span in spans:
        cross = lax.dot_general(own_ref[span, :D], feat, contract_last, preferred_element_type=jnp.float32)
        weight = lax.dot_general(own_ref[span, D:], swapped, contract_last, preferred_element_type=jnp.float32)
        mixed = weight * jnp.exp(cross * (1.0 / D) - sq_ref[...] - own_sq[span, :])
        mixed_b = mixed.astype(jnp.bfloat16)
        mix_ref[span, :] = mixed_b
        total[span, :] += jnp.dot(mixed_b, feat, preferred_element_type=jnp.float32)
        col = col + jnp.sum(mixed.reshape(-1, *col.shape), axis=0)
        lanes = mixed[:, :128]
        for start in range(128, mixed.shape[1], 128):
            lanes = lanes + mixed[:, start : start + 128]
        row_sum[span, :] += lanes
    col_ref[...] = col

    @pl.when(j == steps - 1)
    def _():
        piece_rows = rows // NP
        for p in range(NP):
            span = slice(p * piece_rows, (p + 1) * piece_rows)
            row_total = jnp.sum(row_sum[span, :], axis=1, keepdims=True)
            term_ref[p] = scaled(total[span, :] - row_total * own_ref[span, :D].astype(jnp.float32))


def mix(own, units, partner, unit_sq):
    rows, count = own.shape[0], units.shape[0] + partner.shape[0]
    steps = count // TILE_UNITS
    half = steps // 2
    packed_rows = rows // NP + SCALE_ROWS
    return pl.pallas_call(
        functools.partial(mix_kernel, steps=steps),
        grid=(steps,),
        in_specs=[
            pl.BlockSpec((rows, WIDE), lambda j: (0, 0)),
            pl.BlockSpec((TILE_UNITS, WIDE), lambda j: (jnp.minimum(j, half - 1), 0)),
            pl.BlockSpec((TILE_UNITS, WIDE), lambda j: (jnp.maximum(j - half, 0), 0)),
            pl.BlockSpec((1, TILE_UNITS), lambda j: (0, j)),
        ],
        out_specs=[
            pl.BlockSpec((rows, TILE_UNITS), lambda j: (0, j)),
            pl.BlockSpec((NP, packed_rows, D), lambda j: (0, 0, 0)),
            pl.BlockSpec((8, TILE_UNITS), lambda j: (0, j)),
        ],
        out_shape=[
            pltpu.HBM((rows, count), jnp.bfloat16),
            jax.ShapeDtypeStruct((NP, packed_rows, D), jnp.float32),
            jax.ShapeDtypeStruct((8, count), jnp.float32),
        ],
        scratch_shapes=[pltpu.VMEM((rows, D), jnp.float32), pltpu.VMEM((rows, 1), jnp.float32), pltpu.VMEM((rows, 128), jnp.float32)],
        compiler_params=pltpu.CompilerParams(
            vmem_limit_bytes=24 * 2**20, dimension_semantics=("arbitrary",)
        ),
        cost_estimate=pl.CostEstimate(
            flops=2 * rows * count * (WIDE + D),
            bytes_accessed=2 * rows * count + 2 * WIDE * (rows + count) + 4 * rows * D,
            transcendentals=rows * count,
        ),
    )(own, in_hbm(units), partner, unit_sq)


def local_kernel(mix_ref, own_ref, unit_ref, col_ref, *rest, scale):
    contract_first = (((0,), (0,)), ((), ()))
    out = lax.dot_general(mix_ref[...], own_ref[:, :D], contract_first, preferred_element_type=jnp.float32)
    total = jnp.sum(col_ref[...].T, axis=1, keepdims=True)
    out = out - total * unit_ref[:, :D].astype(jnp.float32)
    if len(rest) == 2:
        out = (out + rest[0][...]) * scale
    rest[-1][...] = out


def local_terms(mixed, own, units, col, first, received=None, scale=1.0):
    rows, count = own.shape[0], units.shape[0]
    base = first // TILE_UNITS
    specs = [
        pl.BlockSpec((rows, TILE_UNITS), lambda j: (0, j + base)),
        pl.BlockSpec((rows, WIDE), lambda j: (0, 0)),
        pl.BlockSpec((TILE_UNITS, WIDE), lambda j: (j, 0)),
        pl.BlockSpec((8, TILE_UNITS), lambda j: (0, j + base)),
    ]
    args = [in_hbm(mixed), own, units, col]
    if received is not None:
        specs.append(pl.BlockSpec((TILE_UNITS, D), lambda j: (j, 0)))
        args.append(received)
    return pl.pallas_call(
        functools.partial(local_kernel, scale=scale),
        grid=(count // TILE_UNITS,),
        in_specs=specs,
        out_specs=pl.BlockSpec((TILE_UNITS, D), lambda j: (j, 0)),
        out_shape=pltpu.HBM((count, D), jnp.float32),
        compiler_params=pltpu.CompilerParams(
            vmem_limit_bytes=24 * 2**20, dimension_semantics=("arbitrary",)
        ),
        cost_estimate=pl.CostEstimate(
            flops=2 * rows * count * D, bytes_accessed=2 * rows * count + 8 * count * D, transcendentals=0
        ),
    )(*args)


def local(unit_data, owner):
    rows = unit_data.shape[0]
    own, partner, squares = broadcast_half(unit_data, owner[0])
    half_rows = own.shape[0]
    mixed, term, col = mix(own, unit_data, partner, squares)
    pieces = exchange(term.astype(jnp.float16))
    away = local_terms(mixed, own, partner, col, rows)
    pieces, away = tie(pieces, away)
    received = swap(away)
    piece = join(*all_w(jnp.sum(unpack(pieces), axis=0)))
    mine = exchange(repeat(piece.astype(jnp.float16)))
    local_grad = local_terms(mixed, own, in_hbm(unit_data), col, 0, received, 1.0 / math.sqrt(rows))
    mine, local_grad = tie(mine, local_grad)
    other = swap(mine)
    first = lax.axis_index("c") == 0
    packed = jnp.concatenate([jnp.where(first, mine, other), jnp.where(first, other, mine)], axis=0)
    owner_grad = unpack(packed, 1.0 / math.sqrt(rows * NP * NW * NC)).reshape(rows, D)
    return (owner_grad, local_grad)


def solution(mesh):
    grid = Mesh(np.asarray(mesh.devices).reshape(NY, NX, NW, NV, NC), ALL)
    in_specs = (P(ALL, None), P())
    out_specs = (P(), P(ALL, None))
    return jax.shard_map(local, mesh=grid, in_specs=in_specs, out_specs=out_specs, check_vma=False)
```

```python
import functools
import math

import jax
import jax.numpy as jnp
import numpy as np
from jax import lax
from jax.experimental import pallas as pl
from jax.experimental.pallas import tpu as pltpu
from jax.sharding import Mesh
from jax.sharding import PartitionSpec as P

D = 256
COLS = 64
WIDE = D + 2 * COLS
PLANE = ("y", "x", "v")
ALL = ("y", "x", "w", "v", "c")
NY, NX, NW, NV, NC = 4, 4, 4, 2, 2
NP = NY * NX * NV
TILE_OWNER = 256
SCALE_ROWS = 8
SMALL = 4 * 2**20


def swap(v):
    return lax.ppermute(v, "c", [(0, 1), (1, 0)])


def shift(v, k):
    return lax.ppermute(v, "w", [(i, (i + k) % NW) for i in range(NW)])


def exchange(v):
    return lax.all_to_all(v, PLANE, 0, 0, tiled=True)


def pick(v, parts, start):
    rows = v.shape[0] // parts
    return lax.dynamic_slice(v, (start, 0), (rows, v.shape[1]), allow_negative_indices=False)


def repeat(v):
    return jnp.broadcast_to(v[None], (NP, *v.shape))


def along_w(v, root):
    away = (lax.axis_index("w") - root) % NW
    up, down, two = shift(v, 1), shift(v, -1), shift(v, 2)
    return jnp.where(away == 0, v, jnp.where(away == 1, up, jnp.where(away == 3, down, two)))


def all_w(v):
    return v, shift(v, 2), shift(v, 1), shift(v, -1)


def in_hbm(v):
    return pltpu.with_memory_space_constraint(v, pltpu.HBM)


def tie(*values):
    return lax.optimization_barrier(values)


def split_kernel(block_ref, here_ref, there_ref, sems):
    rows = here_ref.shape[0]
    core = lax.axis_index("c")
    copies = [
        pltpu.make_async_copy(
            block_ref.at[pl.ds(pl.multiple_of(index * rows, rows), rows)], target, sems.at[slot]
        )
        for slot, (index, target) in enumerate(((1 - core, there_ref), (core, here_ref)))
    ]
    for copy in copies:
        copy.start()
    for copy in copies:
        copy.wait()


def split(block):
    half = jax.ShapeDtypeStruct((block.shape[0] // NC, block.shape[1]), block.dtype)
    return pl.pallas_call(
        split_kernel,
        in_specs=[pl.BlockSpec(memory_space=pl.ANY)],
        out_specs=[pl.BlockSpec(memory_space=pltpu.VMEM)] * 2,
        out_shape=[half, half],
        scratch_shapes=[pltpu.SemaphoreType.DMA((2,))],
        compiler_params=pltpu.CompilerParams(vmem_limit_bytes=SMALL),
    )(in_hbm(block))


def broadcast_half(block, owner):
    here, there = split(block)
    level = owner // NC % (NW * NV)
    start = (owner // (NC * NW * NV) * NV + level % NV) * (here.shape[0] // NP)
    here, other, level, start = tie(here, swap(there), level, start)
    half = jnp.where(owner % NC == lax.axis_index("c"), here, other)
    piece = pick(exchange(half), NP, start)
    parts = (here, there, other, swap(here))
    piece = along_w(piece, level // NV)
    squares = jnp.concatenate([squared(part) for part in parts])[None, :]
    piece, squares, *parts = tie(piece, squares, *parts)
    return exchange(repeat(piece)).reshape(half.shape), parts, squares


def squared(block):
    wide = block[:, :D].astype(jnp.float32)
    return jnp.sum(wide * wide, axis=1) * (0.5 / D)


def scaling(top):
    power = jnp.floor(jnp.log2(jnp.maximum(jnp.max(top, axis=(0, 1), keepdims=True), 1e-30))) - 13.0
    return power, jnp.exp(power * -math.log(2.0))


def sum_pieces(v):
    groups = v.reshape(v.shape[0], -1, SCALE_ROWS, D).astype(jnp.float32)
    powers = groups[:, -1]
    piece = jnp.sum(groups[:, :-1] * jnp.exp2(powers)[:, None], axis=0)
    return jnp.concatenate([piece, jnp.max(powers, axis=0)[None]], axis=0).reshape(-1, D)


def join_kernel(*refs):
    parts, piece_ref, power_ref = refs[:-2], refs[-2], refs[-1]
    rows = piece_ref.shape[0]
    piece = (parts[0][:rows] + parts[1][:rows]) + (parts[2][:rows] + parts[3][:rows])
    power = jnp.maximum(
        jnp.maximum(parts[0][rows:], parts[1][rows:]), jnp.maximum(parts[2][rows:], parts[3][rows:])
    ) + math.log2(NP * NW)
    factor = jnp.exp(power * -math.log(2.0))
    piece_ref[...] = (piece.reshape(-1, SCALE_ROWS, D) * factor[None]).reshape(rows, D)
    power_ref[...] = power


def join(*parts):
    rows = parts[0].shape[0] - SCALE_ROWS
    return pl.pallas_call(
        join_kernel,
        out_shape=[
            jax.ShapeDtypeStruct((rows, D), jnp.float32),
            jax.ShapeDtypeStruct((SCALE_ROWS, D), jnp.float32),
        ],
        compiler_params=pltpu.CompilerParams(vmem_limit_bytes=SMALL),
    )(*parts)


def unscale(v, power, factor):
    groups = v.reshape(-1, SCALE_ROWS, D).astype(jnp.float32) * (jnp.exp2(power) * factor)
    return groups.reshape(-1, D)


def choose(step, refs):
    picked = refs[-1][...]
    for index in range(len(refs) - 1):
        picked = jnp.where(step == index, refs[index][...], picked)
    return picked


def mix_kernel(own_ref, a_ref, b_ref, c_ref, d_ref, sq_ref, mix_ref, term_ref, col_ref, total, own_sq, row_sum, *, steps):
    j = pl.program_id(0)
    rows = own_ref.shape[0]
    spans = [slice(i, i + TILE_OWNER) for i in range(0, rows, TILE_OWNER)]

    @pl.when(j == 0)
    def _():
        total[...] = jnp.zeros_like(total)
        row_sum[...] = jnp.zeros_like(row_sum)
        for span in spans:
            feat = own_ref[span, :D].astype(jnp.float32)
            own_sq[span, :] = jnp.sum(feat * feat, axis=1, keepdims=True) * (0.5 / D) + math.log(2.0 * math.sqrt(COLS))

    units = choose(j, (a_ref, b_ref, c_ref, d_ref))
    feat = units[:, :D]
    swapped = jnp.concatenate([units[:, D + COLS :], units[:, D : D + COLS]], axis=1)
    col = jnp.zeros(col_ref.shape, jnp.float32)
    contract_last = (((1,), (1,)), ((), ()))
    for span in spans:
        cross = lax.dot_general(own_ref[span, :D], feat, contract_last, preferred_element_type=jnp.float32)
        weight = lax.dot_general(own_ref[span, D:], swapped, contract_last, preferred_element_type=jnp.float32)
        mixed = weight * jnp.exp(cross * (1.0 / D) - sq_ref[...] - own_sq[span, :])
        mixed_b = mixed.astype(jnp.bfloat16)
        mix_ref[span, :] = mixed_b
        total[span, :] += jnp.dot(mixed_b, feat, preferred_element_type=jnp.float32)
        col = col + jnp.sum(mixed.reshape(-1, *col.shape), axis=0)
        lanes = mixed[:, :128]
        for start in range(128, mixed.shape[1], 128):
            lanes = lanes + mixed[:, start : start + 128]
        row_sum[span, :] += lanes
    col_ref[...] = col

    @pl.when(j == steps - 1)
    def _():
        top = jnp.zeros((8, D), jnp.float32)
        for span in spans:
            row_total = jnp.sum(row_sum[span, :], axis=1, keepdims=True)
            part = total[span, :] - row_total * own_ref[span, :D].astype(jnp.float32)
            total[span, :] = part
            top = jnp.maximum(top, jnp.max(jnp.abs(part).reshape(-1, 8, D), axis=0))
        power, factor = scaling(top)
        piece_rows = rows // NP
        for p in range(NP):
            term_ref[p, :piece_rows] = total[p * piece_rows : (p + 1) * piece_rows, :] * factor
            term_ref[p, piece_rows:] = jnp.broadcast_to(power, (SCALE_ROWS, D))


def mix(own, parts, unit_sq):
    rows, tile = own.shape[0], parts[0].shape[0]
    steps = len(parts)
    count = steps * tile
    packed_rows = rows // NP + SCALE_ROWS
    return pl.pallas_call(
        functools.partial(mix_kernel, steps=steps),
        grid=(steps,),
        in_specs=[pl.BlockSpec(memory_space=pltpu.VMEM)] * (1 + steps) + [pl.BlockSpec((1, tile), lambda j: (0, j))],
        out_specs=[
            pl.BlockSpec((rows, tile), lambda j: (0, j)),
            pl.BlockSpec((NP, packed_rows, D), lambda j: (0, 0, 0)),
            pl.BlockSpec((8, tile), lambda j: (0, j)),
        ],
        out_shape=[
            pltpu.HBM((rows, count), jnp.bfloat16),
            jax.ShapeDtypeStruct((NP, packed_rows, D), jnp.float32),
            jax.ShapeDtypeStruct((8, count), jnp.float32),
        ],
        scratch_shapes=[pltpu.VMEM((rows, D), jnp.float32), pltpu.VMEM((rows, 1), jnp.float32), pltpu.VMEM((rows, 128), jnp.float32)],
        compiler_params=pltpu.CompilerParams(
            vmem_limit_bytes=24 * 2**20, dimension_semantics=("arbitrary",)
        ),
        cost_estimate=pl.CostEstimate(
            flops=2 * rows * count * (WIDE + D),
            bytes_accessed=2 * rows * count + 2 * WIDE * (rows + count) + 4 * rows * D,
            transcendentals=rows * count,
        ),
    )(own, *parts, unit_sq)


def local_kernel(core_ref, mix_ref, own_ref, a_ref, b_ref, col_ref, *rest, scale):
    contract_first = (((0,), (0,)), ((), ()))
    out = lax.dot_general(mix_ref[...], own_ref[:, :D], contract_first, preferred_element_type=jnp.float32)
    total = jnp.sum(col_ref[...].T, axis=1, keepdims=True)
    units = choose(pl.program_id(0), (a_ref, b_ref))
    out = out - total * units[:, :D].astype(jnp.float32)
    if len(rest) == 2:
        out = (out + rest[0][...]) * scale
    rest[-1][...] = out


def local_terms(core, mixed, own, parts, col, first, received=None, scale=1.0):
    rows, tile = own.shape[0], parts[0].shape[0]
    count = len(parts) * tile
    whole = pl.BlockSpec(memory_space=pltpu.VMEM)
    ordered = pl.BlockSpec((tile, D), lambda j, core: (jnp.where(j == 0, core[0], 1 - core[0]), 0))
    more = [] if received is None else [received]
    return pl.pallas_call(
        functools.partial(local_kernel, scale=scale),
        grid_spec=pltpu.PrefetchScalarGridSpec(
            num_scalar_prefetch=1,
            grid=(len(parts),),
            in_specs=[
                pl.BlockSpec((rows, tile), lambda j, core: (0, j + first)),
                whole,
                whole,
                whole,
                pl.BlockSpec((8, tile), lambda j, core: (0, j + first)),
            ]
            + [ordered] * len(more),
            out_specs=ordered,
        ),
        out_shape=pltpu.HBM((count, D), jnp.float32),
        compiler_params=pltpu.CompilerParams(
            vmem_limit_bytes=24 * 2**20, dimension_semantics=("arbitrary",)
        ),
        cost_estimate=pl.CostEstimate(
            flops=2 * rows * count * D, bytes_accessed=2 * rows * count + 8 * count * D, transcendentals=0
        ),
    )(core, in_hbm(mixed), own, *parts, col, *more)


def place_kernel(mine_ref, other_ref, out_ref, sems):
    rows = mine_ref.shape[0]
    core = lax.axis_index("c")
    copies = [
        pltpu.make_async_copy(source, out_ref.at[pl.ds(pl.multiple_of(index * rows, rows), rows)], sems.at[slot])
        for slot, (index, source) in enumerate(((core, mine_ref), (1 - core, other_ref)))
    ]
    for copy in copies:
        copy.start()
    for copy in copies:
        copy.wait()


def place(mine, other):
    return pl.pallas_call(
        place_kernel,
        in_specs=[pl.BlockSpec(memory_space=pltpu.VMEM)] * 2,
        out_specs=pl.BlockSpec(memory_space=pl.ANY),
        out_shape=jax.ShapeDtypeStruct((NC * mine.shape[0], mine.shape[1]), mine.dtype),
        scratch_shapes=[pltpu.SemaphoreType.DMA((2,))],
        compiler_params=pltpu.CompilerParams(vmem_limit_bytes=SMALL),
    )(mine, other)


def local(unit_data, owner):
    rows = unit_data.shape[0]
    core = lax.axis_index("c").astype(jnp.int32).reshape(1)
    own, parts, squares = broadcast_half(unit_data, owner[0])
    mixed, term, col = mix(own, parts, squares)
    pieces = exchange(term.astype(jnp.float16))
    away = local_terms(core, mixed, own, parts[2:], col, 2)
    pieces, away = tie(pieces, away)
    received = swap(away)
    piece, power = join(*all_w(sum_pieces(pieces)))
    power_other = swap(power)
    mine = exchange(repeat(piece.astype(jnp.float16)))
    local_grad = local_terms(core, mixed, own, parts[:2], col, 0, received, 1.0 / math.sqrt(rows))
    mine, local_grad = tie(mine, local_grad)
    other = swap(mine)
    factor = 1.0 / math.sqrt(rows * NP * NW * NC)
    owner_grad = place(unscale(mine, power, factor), unscale(other, power_other, factor))
    return (owner_grad, local_grad)


def solution(mesh):
    grid = Mesh(np.asarray(mesh.devices).reshape(NY, NX, NW, NV, NC), ALL)
    in_specs = (P(ALL, None), P())
    out_specs = (P(), P(ALL, None))
    return jax.shard_map(local, mesh=grid, in_specs=in_specs, out_specs=out_specs, check_vma=False)
```

```python
import functools
import math

import jax
import jax.numpy as jnp
import numpy as np
from jax import lax
from jax.experimental import pallas as pl
from jax.experimental.pallas import tpu as pltpu
from jax.sharding import Mesh
from jax.sharding import PartitionSpec as P

D = 256
COLS = 64
WIDE = D + 2 * COLS
PLANE = ("x", "v", "y")
ALL = ("y", "x", "w", "v", "c")
NY, NX, NW, NV, NC = 4, 4, 4, 2, 2
NP = NY * NX * NV
TILE_OWNER = 512
CHUNK = 512
SCALE_ROWS = 8
SMALL = 4 * 2**20


def swap(v):
    return lax.ppermute(v, "c", [(0, 1), (1, 0)])


def shift(v, k):
    return lax.ppermute(v, "w", [(i, (i + k) % NW) for i in range(NW)])


def exchange(v):
    return lax.all_to_all(v, PLANE, 0, 0, tiled=True)


def pick(v, parts, start):
    rows = v.shape[0] // parts
    return lax.dynamic_slice(v, (start, 0), (rows, v.shape[1]), allow_negative_indices=False)


def repeat(v):
    return jnp.broadcast_to(v[None], (NP, *v.shape))


def along_w(v, root):
    away = (lax.axis_index("w") - root) % NW
    up, down, two = shift(v, 1), shift(v, -1), shift(v, 2)
    return jnp.where(away == 0, v, jnp.where(away == 1, up, jnp.where(away == 3, down, two)))


def all_w(v):
    return v, shift(v, 2), shift(v, 1), shift(v, -1)


def in_hbm(v):
    return pltpu.with_memory_space_constraint(v, pltpu.HBM)


def tie(*values):
    return lax.optimization_barrier(values)


def part_kernel(block_ref, part_ref, sem, *, mine):
    rows = part_ref.shape[0]
    core = lax.axis_index("c")
    first = pl.multiple_of((core if mine else 1 - core) * rows, rows)
    copy = pltpu.make_async_copy(block_ref.at[pl.ds(first, rows)], part_ref, sem)
    copy.start()
    copy.wait()


def part(block, mine):
    return pl.pallas_call(
        functools.partial(part_kernel, mine=mine),
        in_specs=[pl.BlockSpec(memory_space=pl.ANY)],
        out_specs=pl.BlockSpec(memory_space=pltpu.VMEM),
        out_shape=jax.ShapeDtypeStruct((block.shape[0] // NC, block.shape[1]), block.dtype),
        scratch_shapes=[pltpu.SemaphoreType.DMA],
        compiler_params=pltpu.CompilerParams(vmem_limit_bytes=SMALL),
    )(in_hbm(block))


def broadcast_half(block, owner):
    there, here = part(block, False), part(block, True)
    level = owner // NC % (NW * NV)
    chip = owner // (NC * NW * NV)
    at = {"y": (chip // NX, NY), "x": (chip % NX, NX), "v": (level % NV, NV)}
    start = 0
    for axis in PLANE:
        start = start * at[axis][1] + at[axis][0]
    start = start * (here.shape[0] // NP)
    here, other, level, start = tie(here, swap(there), level, start)
    half = jnp.where(owner % NC == lax.axis_index("c"), here, other)
    (piece,) = tie(pick(exchange(half), NP, start))
    parts = (here, there, other, swap(here))
    piece = along_w(piece, level // NV)
    squares = jnp.concatenate([squared(part) for part in parts])[None, :]
    piece, squares, *parts = tie(piece, squares, *parts)
    return exchange(repeat(piece)).reshape(half.shape), parts, squares


def squared(block):
    wide = block[:, :D].astype(jnp.float32)
    return jnp.sum(wide * wide, axis=1) * (0.5 / D)


def scaling(top):
    power = jnp.floor(jnp.log2(jnp.maximum(jnp.max(top, axis=(0, 1), keepdims=True), 1e-30))) - 13.0
    return power, jnp.exp(power * -math.log(2.0))


def sum_pieces(v):
    groups = v.reshape(v.shape[0], -1, SCALE_ROWS, D).astype(jnp.float32)
    powers = groups[:, -1]
    piece = jnp.sum(groups[:, :-1] * jnp.exp2(powers)[:, None], axis=0)
    return jnp.concatenate([piece, jnp.max(powers, axis=0)[None]], axis=0).reshape(-1, D)


def join_kernel(*refs):
    parts, piece_ref, power_ref = refs[:-2], refs[-2], refs[-1]
    rows = piece_ref.shape[0]
    piece = (parts[0][:rows] + parts[1][:rows]) + (parts[2][:rows] + parts[3][:rows])
    power = jnp.maximum(
        jnp.maximum(parts[0][rows:], parts[1][rows:]), jnp.maximum(parts[2][rows:], parts[3][rows:])
    ) + math.log2(NP * NW)
    factor = jnp.exp(power * -math.log(2.0))
    piece_ref[...] = (piece.reshape(-1, SCALE_ROWS, D) * factor[None]).reshape(rows, D)
    power_ref[...] = power


def join(*parts):
    rows = parts[0].shape[0] - SCALE_ROWS
    return pl.pallas_call(
        join_kernel,
        out_shape=[
            jax.ShapeDtypeStruct((rows, D), jnp.float32),
            jax.ShapeDtypeStruct((SCALE_ROWS, D), jnp.float32),
        ],
        compiler_params=pltpu.CompilerParams(vmem_limit_bytes=SMALL),
    )(*parts)


def unscale(v, power, factor):
    groups = v.reshape(-1, SCALE_ROWS, D).astype(jnp.float32) * (jnp.exp2(power) * factor)
    return groups.reshape(-1, D)


def choose(step, refs):
    picked = refs[-1][...]
    for index in range(len(refs) - 1):
        picked = jnp.where(step == index, refs[index][...], picked)
    return picked


def mix_kernel(own_ref, a_ref, b_ref, c_ref, d_ref, sq_ref, mix_ref, term_ref, col_ref, total, own_sq, row_sum, *, steps):
    j = pl.program_id(0)
    rows = own_ref.shape[0]
    spans = [slice(i, i + TILE_OWNER) for i in range(0, rows, TILE_OWNER)]

    @pl.when(j == 0)
    def _():
        total[...] = jnp.zeros_like(total)
        row_sum[...] = jnp.zeros_like(row_sum)
        for span in spans:
            feat = own_ref[span, :D].astype(jnp.float32)
            own_sq[span, :] = jnp.sum(feat * feat, axis=1, keepdims=True) * (0.5 / D) + math.log(2.0 * math.sqrt(COLS))

    units = choose(j, (a_ref, b_ref, c_ref, d_ref))
    contract_last = (((1,), (1,)), ((), ()))
    chunks = [slice(i, i + CHUNK) for i in range(0, units.shape[0], CHUNK)]
    feats = [units[chunk, :D] for chunk in chunks]
    swapped = [jnp.concatenate([units[chunk, D + COLS :], units[chunk, D : D + COLS]], axis=1) for chunk in chunks]
    cols = [jnp.zeros((8, CHUNK), jnp.float32) for _ in chunks]
    for span in spans:
        lanes = row_sum[span, :]
        for k, chunk in enumerate(chunks):
            cross = lax.dot_general(own_ref[span, :D], feats[k], contract_last, preferred_element_type=jnp.float32)
            weight = lax.dot_general(own_ref[span, D:], swapped[k], contract_last, preferred_element_type=jnp.float32)
            mixed = weight * jnp.exp(cross * (1.0 / D) - sq_ref[:, chunk] - own_sq[span, :])
            mix_ref[span, chunk] = mixed.astype(jnp.bfloat16)
            cols[k] = cols[k] + jnp.sum(mixed.reshape(-1, 8, CHUNK), axis=0)
            for start in range(0, CHUNK, 128):
                lanes = lanes + mixed[:, start : start + 128]
        row_sum[span, :] = lanes
        total[span, :] += jnp.dot(mix_ref[span, :], units[:, :D], preferred_element_type=jnp.float32)
    for k, chunk in enumerate(chunks):
        col_ref[:, chunk] = cols[k]

    @pl.when(j == steps - 1)
    def _():
        top = jnp.zeros((8, D), jnp.float32)
        for span in spans:
            row_total = jnp.sum(row_sum[span, :], axis=1, keepdims=True)
            part = total[span, :] - row_total * own_ref[span, :D].astype(jnp.float32)
            total[span, :] = part
            top = jnp.maximum(top, jnp.max(jnp.abs(part).reshape(-1, 8, D), axis=0))
        power, factor = scaling(top)
        piece_rows = rows // NP
        for p in range(NP):
            term_ref[p, :piece_rows] = total[p * piece_rows : (p + 1) * piece_rows, :] * factor
            term_ref[p, piece_rows:] = jnp.broadcast_to(power, (SCALE_ROWS, D))


def mix(own, parts, unit_sq):
    rows, tile = own.shape[0], parts[0].shape[0]
    steps = len(parts)
    count = steps * tile
    packed_rows = rows // NP + SCALE_ROWS
    return pl.pallas_call(
        functools.partial(mix_kernel, steps=steps),
        grid=(steps,),
        in_specs=[pl.BlockSpec(memory_space=pltpu.VMEM)] * (1 + steps) + [pl.BlockSpec((1, tile), lambda j: (0, j))],
        out_specs=[
            pl.BlockSpec((rows, tile), lambda j: (0, j)),
            pl.BlockSpec((NP, packed_rows, D), lambda j: (0, 0, 0)),
            pl.BlockSpec((8, tile), lambda j: (0, j)),
        ],
        out_shape=[
            pltpu.HBM((rows, count), jnp.bfloat16),
            jax.ShapeDtypeStruct((NP, packed_rows, D), jnp.float32),
            jax.ShapeDtypeStruct((8, count), jnp.float32),
        ],
        scratch_shapes=[pltpu.VMEM((rows, D), jnp.float32), pltpu.VMEM((rows, 1), jnp.float32), pltpu.VMEM((rows, 128), jnp.float32)],
        compiler_params=pltpu.CompilerParams(
            vmem_limit_bytes=24 * 2**20, dimension_semantics=("arbitrary",)
        ),
        cost_estimate=pl.CostEstimate(
            flops=2 * rows * count * (WIDE + D),
            bytes_accessed=2 * rows * count + 2 * WIDE * (rows + count) + 4 * rows * D,
            transcendentals=rows * count,
        ),
    )(own, *parts, unit_sq)


def local_kernel(core_ref, mix_ref, own_ref, a_ref, b_ref, col_ref, *rest, scale):
    contract_first = (((0,), (0,)), ((), ()))
    out = lax.dot_general(mix_ref[...], own_ref[:, :D], contract_first, preferred_element_type=jnp.float32)
    total = jnp.sum(col_ref[...].T, axis=1, keepdims=True)
    units = choose(pl.program_id(0), (a_ref, b_ref))
    out = out - total * units[:, :D].astype(jnp.float32)
    if len(rest) == 2:
        out = (out + rest[0][...]) * scale
    rest[-1][...] = out


def local_terms(core, mixed, own, parts, col, first, received=None, scale=1.0):
    rows, tile = own.shape[0], parts[0].shape[0]
    count = len(parts) * tile
    whole = pl.BlockSpec(memory_space=pltpu.VMEM)
    ordered = pl.BlockSpec((tile, D), lambda j, core: (jnp.where(j == 0, core[0], 1 - core[0]), 0))
    more = [] if received is None else [received]
    return pl.pallas_call(
        functools.partial(local_kernel, scale=scale),
        grid_spec=pltpu.PrefetchScalarGridSpec(
            num_scalar_prefetch=1,
            grid=(len(parts),),
            in_specs=[
                pl.BlockSpec((rows, tile), lambda j, core: (0, j + first)),
                whole,
                whole,
                whole,
                pl.BlockSpec((8, tile), lambda j, core: (0, j + first)),
            ]
            + [ordered] * len(more),
            out_specs=ordered,
        ),
        out_shape=pltpu.HBM((count, D), jnp.float32),
        compiler_params=pltpu.CompilerParams(
            vmem_limit_bytes=24 * 2**20, dimension_semantics=("arbitrary",)
        ),
        cost_estimate=pl.CostEstimate(
            flops=2 * rows * count * D, bytes_accessed=2 * rows * count + 8 * count * D, transcendentals=0
        ),
    )(core, in_hbm(mixed), own, *parts, col, *more)


def place_kernel(half_ref, *rest, mine):
    out_ref, sem = rest[-2:]
    rows = half_ref.shape[0]
    core = lax.axis_index("c")
    first = pl.multiple_of((core if mine else 1 - core) * rows, rows)
    copy = pltpu.make_async_copy(half_ref, out_ref.at[pl.ds(first, rows)], sem)
    copy.start()
    copy.wait()


def place(half, out=None):
    mine = out is None
    return pl.pallas_call(
        functools.partial(place_kernel, mine=mine),
        in_specs=[pl.BlockSpec(memory_space=pltpu.VMEM)] + [pl.BlockSpec(memory_space=pl.ANY)] * (not mine),
        out_specs=pl.BlockSpec(memory_space=pl.ANY),
        out_shape=pltpu.HBM((NC * half.shape[0], half.shape[1]), half.dtype),
        scratch_shapes=[pltpu.SemaphoreType.DMA],
        input_output_aliases={} if mine else {1: 0},
        compiler_params=pltpu.CompilerParams(vmem_limit_bytes=SMALL),
    )(half, *([] if mine else [out]))


def local(unit_data, owner):
    rows = unit_data.shape[0]
    core = lax.axis_index("c").astype(jnp.int32).reshape(1)
    own, parts, squares = broadcast_half(unit_data, owner[0])
    mixed, term, col = mix(own, parts, squares)
    pieces = exchange(term.astype(jnp.float16))
    away = local_terms(core, mixed, own, parts[2:], col, 2)
    pieces, away = tie(pieces, away)
    received = swap(away)
    piece, power = join(*all_w(sum_pieces(pieces)))
    power_other = swap(power)
    mine = exchange(repeat(piece.astype(jnp.float16)))
    local_grad = local_terms(core, mixed, own, parts[:2], col, 0, received, 1.0 / math.sqrt(rows))
    mine, local_grad = tie(mine, local_grad)
    other = swap(mine)
    factor = 1.0 / math.sqrt(rows * NP * NW * NC)
    owner_grad = place(unscale(other, power_other, factor), place(unscale(mine, power, factor)))
    return (owner_grad, local_grad)


def solution(mesh):
    grid = Mesh(np.asarray(mesh.devices).reshape(NY, NX, NW, NV, NC), ALL)
    in_specs = (P(ALL, None), P())
    out_specs = (P(), P(ALL, None))
    return jax.shard_map(local, mesh=grid, in_specs=in_specs, out_specs=out_specs, check_vma=False)
```

```python
import functools
import math

import jax
import jax.numpy as jnp
import numpy as np
from jax import lax
from jax.experimental import pallas as pl
from jax.experimental.pallas import tpu as pltpu
from jax.sharding import Mesh
from jax.sharding import PartitionSpec as P

D = 256
COLS = 64
WIDE = D + 2 * COLS
PLANE = ("x", "v", "y")
ALL = ("y", "x", "w", "v", "c")
NY, NX, NW, NV, NC = 4, 4, 4, 2, 2
NP = NY * NX * NV
TILE_OWNER = 512
CHUNK = 512
SCALE_ROWS = 8
LANES = 128
SMALL = 4 * 2**20


def swap(v):
    return lax.ppermute(v, "c", [(0, 1), (1, 0)])


def shift(v, k):
    return lax.ppermute(v, "w", [(i, (i + k) % NW) for i in range(NW)])


def exchange(v):
    return lax.all_to_all(v, PLANE, 0, 0, tiled=True)


def pick(v, parts, start):
    rows = v.shape[0] // parts
    return lax.dynamic_slice(v, (start, 0), (rows, v.shape[1]), allow_negative_indices=False)


def repeat(v):
    return jnp.broadcast_to(v[None], (NP, *v.shape))


def along_w(v, root):
    away = (lax.axis_index("w") - root) % NW
    up, down, two = shift(v, 1), shift(v, -1), shift(v, 2)
    return jnp.where(away == 0, v, jnp.where(away == 1, up, jnp.where(away == 3, down, two)))


def all_w(v):
    return v, shift(v, 2), shift(v, 1), shift(v, -1)


def in_hbm(v):
    return pltpu.with_memory_space_constraint(v, pltpu.HBM)


def tie(*values):
    return lax.optimization_barrier(values)


def part_kernel(block_ref, part_ref, sem, *, mine):
    rows = part_ref.shape[0]
    core = lax.axis_index("c")
    first = pl.multiple_of((core if mine else 1 - core) * rows, rows)
    copy = pltpu.make_async_copy(block_ref.at[pl.ds(first, rows)], part_ref, sem)
    copy.start()
    copy.wait()


def part(block, mine):
    return pl.pallas_call(
        functools.partial(part_kernel, mine=mine),
        in_specs=[pl.BlockSpec(memory_space=pl.ANY)],
        out_specs=pl.BlockSpec(memory_space=pltpu.VMEM),
        out_shape=jax.ShapeDtypeStruct((block.shape[0] // NC, block.shape[1]), block.dtype),
        scratch_shapes=[pltpu.SemaphoreType.DMA],
        compiler_params=pltpu.CompilerParams(vmem_limit_bytes=SMALL),
    )(in_hbm(block))


def broadcast_half(block, owner):
    there, here = part(block, False), part(block, True)
    level = owner // NC % (NW * NV)
    chip = owner // (NC * NW * NV)
    at = {"y": (chip // NX, NY), "x": (chip % NX, NX), "v": (level % NV, NV)}
    start = 0
    for axis in PLANE:
        start = start * at[axis][1] + at[axis][0]
    start = start * (here.shape[0] // NP)
    here, other, level, start = tie(here, swap(there), level, start)
    half = jnp.where(owner % NC == lax.axis_index("c"), here, other)
    (piece,) = tie(pick(exchange(half), NP, start))
    parts = (here, there, other, swap(here))
    piece = along_w(piece, level // NV)
    squares = jnp.concatenate([squared(part) for part in parts])[None, :]
    piece, squares, *parts = tie(piece, squares, *parts)
    return exchange(repeat(piece)).reshape(half.shape), parts, squares


def squared(block):
    wide = block[:, :D].astype(jnp.float32)
    return jnp.sum(wide * wide, axis=1) * (0.5 / D)


def scaling(top):
    power = jnp.floor(jnp.log2(jnp.maximum(jnp.max(top, axis=(0, 1), keepdims=True), 1e-30))) - 13.0
    return power, jnp.exp(power * -math.log(2.0))


def sum_pieces(v):
    groups = v.reshape(v.shape[0], -1, SCALE_ROWS, LANES).astype(jnp.float32)
    powers = groups[:, -1]
    piece = jnp.sum(groups[:, :-1] * jnp.exp2(powers)[:, None], axis=0)
    return jnp.concatenate([piece, jnp.max(powers, axis=0)[None]], axis=0).reshape(-1, LANES)


def join_kernel(*refs):
    parts, piece_ref, power_ref = refs[:-2], refs[-2], refs[-1]
    rows = parts[0].shape[0] - SCALE_ROWS
    piece = (parts[0][:rows] + parts[1][:rows]) + (parts[2][:rows] + parts[3][:rows])
    power = jnp.maximum(
        jnp.maximum(parts[0][rows:], parts[1][rows:]), jnp.maximum(parts[2][rows:], parts[3][rows:])
    ) + math.log2(NP * NW)
    factor = jnp.exp(power * -math.log(2.0))
    piece = (piece.reshape(-1, SCALE_ROWS, LANES) * factor[None]).reshape(rows, LANES)
    height = piece_ref.shape[0]
    for k in range(D // LANES):
        piece_ref[:, k * LANES : (k + 1) * LANES] = piece[k * height : (k + 1) * height]
        power_ref[:, k * LANES : (k + 1) * LANES] = power


def join(*parts):
    rows = (parts[0].shape[0] - SCALE_ROWS) * LANES // D
    return pl.pallas_call(
        join_kernel,
        out_shape=[
            jax.ShapeDtypeStruct((rows, D), jnp.float32),
            jax.ShapeDtypeStruct((SCALE_ROWS, D), jnp.float32),
        ],
        compiler_params=pltpu.CompilerParams(vmem_limit_bytes=SMALL),
    )(*parts)


def unscale(v, power, factor):
    groups = v.reshape(-1, SCALE_ROWS, D).astype(jnp.float32) * (jnp.exp2(power) * factor)
    return groups.reshape(-1, D)


def choose(step, refs):
    picked = refs[-1][...]
    for index in range(len(refs) - 1):
        picked = jnp.where(step == index, refs[index][...], picked)
    return picked


def mix_kernel(own_ref, a_ref, b_ref, c_ref, d_ref, sq_ref, mix_ref, term_ref, col_ref, total, own_sq, row_sum, *, steps):
    j = pl.program_id(0)
    rows = own_ref.shape[0]
    spans = [slice(i, i + TILE_OWNER) for i in range(0, rows, TILE_OWNER)]

    @pl.when(j == 0)
    def _():
        total[...] = jnp.zeros_like(total)
        row_sum[...] = jnp.zeros_like(row_sum)
        for span in spans:
            feat = own_ref[span, :D].astype(jnp.float32)
            own_sq[span, :] = jnp.sum(feat * feat, axis=1, keepdims=True) * (0.5 / D) + math.log(2.0 * math.sqrt(COLS))

    units = choose(j, (a_ref, b_ref, c_ref, d_ref))
    contract_last = (((1,), (1,)), ((), ()))
    chunks = [slice(i, i + CHUNK) for i in range(0, units.shape[0], CHUNK)]
    feats = [units[chunk, :D] for chunk in chunks]
    swapped = [jnp.concatenate([units[chunk, D + COLS :], units[chunk, D : D + COLS]], axis=1) for chunk in chunks]
    cols = [jnp.zeros((8, CHUNK), jnp.float32) for _ in chunks]
    for span in spans:
        lanes = row_sum[span, :]
        for k, chunk in enumerate(chunks):
            cross = lax.dot_general(own_ref[span, :D], feats[k], contract_last, preferred_element_type=jnp.float32)
            weight = lax.dot_general(own_ref[span, D:], swapped[k], contract_last, preferred_element_type=jnp.float32)
            mixed = weight * jnp.exp(cross * (1.0 / D) - sq_ref[:, chunk] - own_sq[span, :])
            mix_ref[span, chunk] = mixed.astype(jnp.bfloat16)
            cols[k] = cols[k] + jnp.sum(mixed.reshape(-1, 8, CHUNK), axis=0)
            for start in range(0, CHUNK, 128):
                lanes = lanes + mixed[:, start : start + 128]
        row_sum[span, :] = lanes
        total[span, :] += jnp.dot(mix_ref[span, :], units[:, :D], preferred_element_type=jnp.float32)
    for k, chunk in enumerate(chunks):
        col_ref[:, chunk] = cols[k]

    @pl.when(j == steps - 1)
    def _():
        top = jnp.zeros((8, D), jnp.float32)
        for span in spans:
            row_total = jnp.sum(row_sum[span, :], axis=1, keepdims=True)
            part = total[span, :] - row_total * own_ref[span, :D].astype(jnp.float32)
            total[span, :] = part
            top = jnp.maximum(top, jnp.max(jnp.abs(part).reshape(-1, 8, D), axis=0))
        power, factor = scaling(top)
        piece_rows = rows // NP
        for p in range(NP):
            scaled = total[p * piece_rows : (p + 1) * piece_rows, :] * factor
            for k in range(D // LANES):
                term_ref[p, k * piece_rows : (k + 1) * piece_rows] = scaled[:, k * LANES : (k + 1) * LANES]
            term_ref[p, D // LANES * piece_rows :] = jnp.broadcast_to(power, (SCALE_ROWS, LANES))


def mix(own, parts, unit_sq):
    rows, tile = own.shape[0], parts[0].shape[0]
    steps = len(parts)
    count = steps * tile
    packed_rows = D // LANES * rows // NP + SCALE_ROWS
    return pl.pallas_call(
        functools.partial(mix_kernel, steps=steps),
        grid=(steps,),
        in_specs=[pl.BlockSpec(memory_space=pltpu.VMEM)] * (1 + steps) + [pl.BlockSpec((1, tile), lambda j: (0, j))],
        out_specs=[
            pl.BlockSpec((rows, tile), lambda j: (0, j)),
            pl.BlockSpec((NP, packed_rows, LANES), lambda j: (0, 0, 0)),
            pl.BlockSpec((8, tile), lambda j: (0, j)),
        ],
        out_shape=[
            pltpu.HBM((rows, count), jnp.bfloat16),
            jax.ShapeDtypeStruct((NP, packed_rows, LANES), jnp.float32),
            jax.ShapeDtypeStruct((8, count), jnp.float32),
        ],
        scratch_shapes=[pltpu.VMEM((rows, D), jnp.float32), pltpu.VMEM((rows, 1), jnp.float32), pltpu.VMEM((rows, 128), jnp.float32)],
        compiler_params=pltpu.CompilerParams(
            vmem_limit_bytes=24 * 2**20, dimension_semantics=("arbitrary",)
        ),
        cost_estimate=pl.CostEstimate(
            flops=2 * rows * count * (WIDE + D),
            bytes_accessed=2 * rows * count + 2 * WIDE * (rows + count) + 4 * rows * D,
            transcendentals=rows * count,
        ),
    )(own, *parts, unit_sq)


def local_kernel(core_ref, mix_ref, own_ref, a_ref, b_ref, col_ref, *rest, scale):
    contract_first = (((0,), (0,)), ((), ()))
    out = lax.dot_general(mix_ref[...], own_ref[:, :D], contract_first, preferred_element_type=jnp.float32)
    total = jnp.sum(col_ref[...].T, axis=1, keepdims=True)
    units = choose(pl.program_id(0), (a_ref, b_ref))
    out = out - total * units[:, :D].astype(jnp.float32)
    if len(rest) == 2:
        out = (out + rest[0][...]) * scale
    rest[-1][...] = out


def local_terms(core, mixed, own, parts, col, first, received=None, scale=1.0):
    rows, tile = own.shape[0], parts[0].shape[0]
    count = len(parts) * tile
    whole = pl.BlockSpec(memory_space=pltpu.VMEM)
    ordered = pl.BlockSpec((tile, D), lambda j, core: (jnp.where(j == 0, core[0], 1 - core[0]), 0))
    more = [] if received is None else [received]
    return pl.pallas_call(
        functools.partial(local_kernel, scale=scale),
        grid_spec=pltpu.PrefetchScalarGridSpec(
            num_scalar_prefetch=1,
            grid=(len(parts),),
            in_specs=[
                pl.BlockSpec((rows, tile), lambda j, core: (0, j + first)),
                whole,
                whole,
                whole,
                pl.BlockSpec((8, tile), lambda j, core: (0, j + first)),
            ]
            + [ordered] * len(more),
            out_specs=ordered,
        ),
        out_shape=pltpu.HBM((count, D), jnp.float32),
        compiler_params=pltpu.CompilerParams(
            vmem_limit_bytes=24 * 2**20, dimension_semantics=("arbitrary",)
        ),
        cost_estimate=pl.CostEstimate(
            flops=2 * rows * count * D, bytes_accessed=2 * rows * count + 8 * count * D, transcendentals=0
        ),
    )(core, in_hbm(mixed), own, *parts, col, *more)


def place_kernel(half_ref, out_ref, sem):
    rows = half_ref.shape[0]
    first = pl.multiple_of(lax.axis_index("c") * rows, rows)
    copy = pltpu.make_async_copy(half_ref, out_ref.at[pl.ds(first, rows)], sem)
    copy.start()
    copy.wait()


def place(half):
    return pl.pallas_call(
        place_kernel,
        in_specs=[pl.BlockSpec(memory_space=pltpu.VMEM)],
        out_specs=pl.BlockSpec(memory_space=pl.ANY),
        out_shape=pltpu.HBM((NC * half.shape[0], half.shape[1]), half.dtype),
        scratch_shapes=[pltpu.SemaphoreType.DMA],
        compiler_params=pltpu.CompilerParams(vmem_limit_bytes=SMALL),
    )(half)


def local(unit_data, owner):
    rows = unit_data.shape[0]
    core = lax.axis_index("c").astype(jnp.int32).reshape(1)
    own, parts, squares = broadcast_half(unit_data, owner[0])
    mixed, term, col = mix(own, parts, squares)
    pieces = exchange(term.astype(jnp.float16))
    away = local_terms(core, mixed, own, parts[2:], col, 2)
    pieces, away = tie(pieces, away)
    received = swap(away)
    piece, power = join(*all_w(sum_pieces(pieces)))
    power_other = swap(power)
    mine = exchange(repeat(piece.astype(jnp.float16)))
    local_grad = local_terms(core, mixed, own, parts[:2], col, 0, received, 1.0 / math.sqrt(rows))
    mine, local_grad = tie(mine, local_grad)
    other = swap(mine)
    factor = 1.0 / math.sqrt(rows * NP * NW * NC)
    first = (1 - lax.axis_index("c")) * (rows // NC)
    owner_grad = lax.dynamic_update_slice(
        place(unscale(mine, power, factor)), unscale(other, power_other, factor), (first, 0), allow_negative_indices=False
    )
    return (owner_grad, local_grad)


def solution(mesh):
    grid = Mesh(np.asarray(mesh.devices).reshape(NY, NX, NW, NV, NC), ALL)
    in_specs = (P(ALL, None), P())
    out_specs = (P(), P(ALL, None))
    return jax.shard_map(local, mesh=grid, in_specs=in_specs, out_specs=out_specs, check_vma=False)
```

```python
import functools
import math

import jax
import jax.numpy as jnp
import numpy as np
from jax import lax
from jax.experimental import pallas as pl
from jax.experimental.pallas import tpu as pltpu
from jax.sharding import Mesh
from jax.sharding import PartitionSpec as P

D = 256
COLS = 64
WIDE = D + 2 * COLS
PLANE = ("x", "v", "y")
ALL = ("y", "x", "w", "v", "c")
NY, NX, NW, NV, NC = 4, 4, 4, 2, 2
NP = NY * NX * NV
TILE_OWNER = 512
CHUNK = 512
SCALE_ROWS = 8
LANES = 128
SMALL = 4 * 2**20


def swap(v):
    return lax.ppermute(v, "c", [(0, 1), (1, 0)])


def shift(v, k):
    return lax.ppermute(v, "w", [(i, (i + k) % NW) for i in range(NW)])


def exchange(v):
    return lax.all_to_all(v, PLANE, 0, 0, tiled=True)


def pick(v, parts, start):
    rows = v.shape[0] // parts
    return lax.dynamic_slice(v, (start, 0), (rows, v.shape[1]), allow_negative_indices=False)


def repeat(v):
    return jnp.broadcast_to(v[None], (NP, *v.shape))


def along_w(v, root):
    away = (lax.axis_index("w") - root) % NW
    up, down, two = shift(v, 1), shift(v, -1), shift(v, 2)
    return jnp.where(away == 0, v, jnp.where(away == 1, up, jnp.where(away == 3, down, two)))


def all_w(v):
    return v, shift(v, 2), shift(v, 1), shift(v, -1)


def in_hbm(v):
    return pltpu.with_memory_space_constraint(v, pltpu.HBM)


def tie(*values):
    return lax.optimization_barrier(values)


def part_kernel(block_ref, part_ref, sem, *, mine):
    rows = part_ref.shape[0]
    core = lax.axis_index("c")
    first = pl.multiple_of((core if mine else 1 - core) * rows, rows)
    copy = pltpu.make_async_copy(block_ref.at[pl.ds(first, rows)], part_ref, sem)
    copy.start()
    copy.wait()


def part(block, mine):
    return pl.pallas_call(
        functools.partial(part_kernel, mine=mine),
        in_specs=[pl.BlockSpec(memory_space=pl.ANY)],
        out_specs=pl.BlockSpec(memory_space=pltpu.VMEM),
        out_shape=jax.ShapeDtypeStruct((block.shape[0] // NC, block.shape[1]), block.dtype),
        scratch_shapes=[pltpu.SemaphoreType.DMA],
        compiler_params=pltpu.CompilerParams(vmem_limit_bytes=SMALL),
    )(in_hbm(block))


def broadcast_half(block, owner):
    there, here = part(block, False), part(block, True)
    level = owner // NC % (NW * NV)
    chip = owner // (NC * NW * NV)
    at = {"y": (chip // NX, NY), "x": (chip % NX, NX), "v": (level % NV, NV)}
    start = 0
    for axis in PLANE:
        start = start * at[axis][1] + at[axis][0]
    start = start * (here.shape[0] // NP)
    here, other, level, start = tie(here, swap(there), level, start)
    half = jnp.where(owner % NC == lax.axis_index("c"), here, other)
    (piece,) = tie(pick(exchange(half), NP, start))
    parts = (here, there, other, swap(here))
    piece = along_w(piece, level // NV)
    squares = jnp.concatenate([squared(part) for part in parts])[None, :]
    piece, squares, *parts = tie(piece, squares, *parts)
    return exchange(repeat(piece)).reshape(half.shape), parts, squares


def squared(block):
    wide = block[:, :D].astype(jnp.float32)
    return jnp.sum(wide * wide, axis=1) * (0.5 / D)


def scaling(top):
    power = jnp.floor(jnp.log2(jnp.maximum(jnp.max(top, axis=(0, 1), keepdims=True), 1e-30))) - 13.0
    return power, jnp.exp(power * -math.log(2.0))


def sum_pieces(v):
    groups = v.reshape(v.shape[0], -1, SCALE_ROWS, LANES).astype(jnp.float32)
    powers = groups[:, -1]
    piece = jnp.sum(groups[:, :-1] * jnp.exp2(powers)[:, None], axis=0)
    return jnp.concatenate([piece, jnp.max(powers, axis=0)[None]], axis=0).reshape(-1, LANES)


def join_kernel(*refs):
    parts, piece_ref, power_ref = refs[:-2], refs[-2], refs[-1]
    rows = parts[0].shape[0] - SCALE_ROWS
    piece = (parts[0][:rows] + parts[1][:rows]) + (parts[2][:rows] + parts[3][:rows])
    power = jnp.maximum(
        jnp.maximum(parts[0][rows:], parts[1][rows:]), jnp.maximum(parts[2][rows:], parts[3][rows:])
    ) + math.log2(NP * NW)
    factor = jnp.exp(power * -math.log(2.0))
    piece = (piece.reshape(-1, SCALE_ROWS, LANES) * factor[None]).reshape(rows, LANES)
    height = piece_ref.shape[0]
    for k in range(D // LANES):
        piece_ref[:, k * LANES : (k + 1) * LANES] = piece[k * height : (k + 1) * height]
        power_ref[:, k * LANES : (k + 1) * LANES] = power


def join(*parts):
    rows = (parts[0].shape[0] - SCALE_ROWS) * LANES // D
    return pl.pallas_call(
        join_kernel,
        out_shape=[
            jax.ShapeDtypeStruct((rows, D), jnp.float32),
            jax.ShapeDtypeStruct((SCALE_ROWS, D), jnp.float32),
        ],
        compiler_params=pltpu.CompilerParams(vmem_limit_bytes=SMALL),
    )(*parts)


def unscale(v, power, factor):
    groups = v.reshape(-1, SCALE_ROWS, D).astype(jnp.float32) * (jnp.exp2(power) * factor)
    return groups.reshape(-1, D)


def choose(step, refs):
    picked = refs[-1][...]
    for index in range(len(refs) - 1):
        picked = jnp.where(step == index, refs[index][...], picked)
    return picked


def mix_kernel(own_ref, a_ref, b_ref, c_ref, d_ref, sq_ref, mix_ref, term_ref, col_ref, total, own_sq, row_sum, *, steps):
    j = pl.program_id(0)
    rows = own_ref.shape[0]
    spans = [slice(i, i + TILE_OWNER) for i in range(0, rows, TILE_OWNER)]

    @pl.when(j == 0)
    def _():
        total[...] = jnp.zeros_like(total)
        row_sum[...] = jnp.zeros_like(row_sum)
        for span in spans:
            feat = own_ref[span, :D].astype(jnp.float32)
            own_sq[span, :] = jnp.sum(feat * feat, axis=1, keepdims=True) * (0.5 / D) + math.log(2.0 * math.sqrt(COLS))

    units = choose(j, (a_ref, b_ref, c_ref, d_ref))
    contract_last = (((1,), (1,)), ((), ()))
    chunks = [slice(i, i + CHUNK) for i in range(0, units.shape[0], CHUNK)]
    feats = [units[chunk, :D] for chunk in chunks]
    swapped = [jnp.concatenate([units[chunk, D + COLS :], units[chunk, D : D + COLS]], axis=1) for chunk in chunks]
    cols = [jnp.zeros((8, CHUNK), jnp.float32) for _ in chunks]
    for span in spans:
        lanes = row_sum[span, :]
        for k, chunk in enumerate(chunks):
            cross = lax.dot_general(own_ref[span, :D], feats[k], contract_last, preferred_element_type=jnp.float32)
            weight = lax.dot_general(own_ref[span, D:], swapped[k], contract_last, preferred_element_type=jnp.float32)
            mixed = weight * jnp.exp(cross * (1.0 / D) - sq_ref[:, chunk] - own_sq[span, :])
            mix_ref[span, chunk] = mixed.astype(jnp.bfloat16)
            cols[k] = cols[k] + jnp.sum(mixed.reshape(-1, 8, CHUNK), axis=0)
            for start in range(0, CHUNK, 128):
                lanes = lanes + mixed[:, start : start + 128]
        row_sum[span, :] = lanes
        total[span, :] += jnp.dot(mix_ref[span, :], units[:, :D], preferred_element_type=jnp.float32)
    for k, chunk in enumerate(chunks):
        col_ref[:, chunk] = cols[k]

    @pl.when(j == steps - 1)
    def _():
        top = jnp.zeros((8, D), jnp.float32)
        for span in spans:
            row_total = jnp.sum(row_sum[span, :], axis=1, keepdims=True)
            part = total[span, :] - row_total * own_ref[span, :D].astype(jnp.float32)
            total[span, :] = part
            top = jnp.maximum(top, jnp.max(jnp.abs(part).reshape(-1, 8, D), axis=0))
        power, factor = scaling(top)
        piece_rows = rows // NP
        for p in range(NP):
            scaled = total[p * piece_rows : (p + 1) * piece_rows, :] * factor
            for k in range(D // LANES):
                term_ref[p, k * piece_rows : (k + 1) * piece_rows] = scaled[:, k * LANES : (k + 1) * LANES]
            term_ref[p, D // LANES * piece_rows :] = jnp.broadcast_to(power, (SCALE_ROWS, LANES))


def mix(own, parts, unit_sq):
    rows, tile = own.shape[0], parts[0].shape[0]
    steps = len(parts)
    count = steps * tile
    packed_rows = D // LANES * rows // NP + SCALE_ROWS
    return pl.pallas_call(
        functools.partial(mix_kernel, steps=steps),
        grid=(steps,),
        in_specs=[pl.BlockSpec(memory_space=pltpu.VMEM)] * (1 + steps) + [pl.BlockSpec((1, tile), lambda j: (0, j))],
        out_specs=[
            pl.BlockSpec((rows, tile), lambda j: (0, j)),
            pl.BlockSpec((NP, packed_rows, LANES), lambda j: (0, 0, 0)),
            pl.BlockSpec((8, tile), lambda j: (0, j)),
        ],
        out_shape=[
            pltpu.HBM((rows, count), jnp.bfloat16),
            jax.ShapeDtypeStruct((NP, packed_rows, LANES), jnp.float32),
            jax.ShapeDtypeStruct((8, count), jnp.float32),
        ],
        scratch_shapes=[pltpu.VMEM((rows, D), jnp.float32), pltpu.VMEM((rows, 1), jnp.float32), pltpu.VMEM((rows, 128), jnp.float32)],
        compiler_params=pltpu.CompilerParams(
            vmem_limit_bytes=14 * 2**20, dimension_semantics=("arbitrary",)
        ),
        cost_estimate=pl.CostEstimate(
            flops=2 * rows * count * (WIDE + D),
            bytes_accessed=2 * rows * count + 2 * WIDE * (rows + count) + 4 * rows * D,
            transcendentals=rows * count,
        ),
    )(own, *parts, unit_sq)


def local_kernel(core_ref, mix_ref, own_ref, a_ref, b_ref, col_ref, *rest, scale):
    contract_first = (((0,), (0,)), ((), ()))
    out = lax.dot_general(mix_ref[...], own_ref[:, :D], contract_first, preferred_element_type=jnp.float32)
    total = jnp.sum(col_ref[...].T, axis=1, keepdims=True)
    units = choose(pl.program_id(0), (a_ref, b_ref))
    out = out - total * units[:, :D].astype(jnp.float32)
    if len(rest) == 2:
        out = (out + rest[0][...]) * scale
    rest[-1][...] = out


def local_terms(core, mixed, own, parts, col, first, received=None, scale=1.0):
    rows, tile = own.shape[0], parts[0].shape[0]
    count = len(parts) * tile
    whole = pl.BlockSpec(memory_space=pltpu.VMEM)
    ordered = pl.BlockSpec((tile, D), lambda j, core: (jnp.where(j == 0, core[0], 1 - core[0]), 0))
    more = [] if received is None else [received]
    return pl.pallas_call(
        functools.partial(local_kernel, scale=scale),
        grid_spec=pltpu.PrefetchScalarGridSpec(
            num_scalar_prefetch=1,
            grid=(len(parts),),
            in_specs=[
                pl.BlockSpec((rows, tile), lambda j, core: (0, j + first)),
                whole,
                whole,
                whole,
                pl.BlockSpec((8, tile), lambda j, core: (0, j + first)),
            ]
            + [ordered] * len(more),
            out_specs=ordered,
        ),
        out_shape=pltpu.HBM((count, D), jnp.float32),
        compiler_params=pltpu.CompilerParams(
            vmem_limit_bytes=14 * 2**20, dimension_semantics=("arbitrary",)
        ),
        cost_estimate=pl.CostEstimate(
            flops=2 * rows * count * D, bytes_accessed=2 * rows * count + 8 * count * D, transcendentals=0
        ),
    )(core, in_hbm(mixed), own, *parts, col, *more)


def place_kernel(half_ref, out_ref, sem):
    rows = half_ref.shape[0]
    first = pl.multiple_of(lax.axis_index("c") * rows, rows)
    copy = pltpu.make_async_copy(half_ref, out_ref.at[pl.ds(first, rows)], sem)
    copy.start()
    copy.wait()


def place(half):
    return pl.pallas_call(
        place_kernel,
        in_specs=[pl.BlockSpec(memory_space=pltpu.VMEM)],
        out_specs=pl.BlockSpec(memory_space=pl.ANY),
        out_shape=pltpu.HBM((NC * half.shape[0], half.shape[1]), half.dtype),
        scratch_shapes=[pltpu.SemaphoreType.DMA],
        compiler_params=pltpu.CompilerParams(vmem_limit_bytes=SMALL),
    )(half)


def local(unit_data, owner):
    rows = unit_data.shape[0]
    core = lax.axis_index("c").astype(jnp.int32).reshape(1)
    own, parts, squares = broadcast_half(unit_data, owner[0])
    mixed, term, col = mix(own, parts, squares)
    pieces = exchange(term.astype(jnp.float16))
    away = local_terms(core, mixed, own, parts[2:], col, 2)
    pieces, away = tie(pieces, away)
    received = swap(away)
    piece, power = join(*all_w(sum_pieces(pieces)))
    power_other = swap(power)
    mine = exchange(repeat(piece.astype(jnp.float16)))
    local_grad = local_terms(core, mixed, own, parts[:2], col, 0, received, 1.0 / math.sqrt(rows))
    mine, local_grad = tie(mine, local_grad)
    other = swap(mine)
    factor = 1.0 / math.sqrt(rows * NP * NW * NC)
    first = (1 - lax.axis_index("c")) * (rows // NC)
    owner_grad = lax.dynamic_update_slice(
        place(unscale(mine, power, factor)), unscale(other, power_other, factor), (first, 0), allow_negative_indices=False
    )
    return (owner_grad, local_grad)


def solution(mesh):
    grid = Mesh(np.asarray(mesh.devices).reshape(NY, NX, NW, NV, NC), ALL)
    in_specs = (P(ALL, None), P())
    out_specs = (P(), P(ALL, None))
    return jax.shard_map(local, mesh=grid, in_specs=in_specs, out_specs=out_specs, check_vma=False)
```

```python
import functools
import math

import jax
import jax.numpy as jnp
import numpy as np
from jax import lax
from jax.experimental import pallas as pl
from jax.experimental.pallas import tpu as pltpu
from jax.sharding import Mesh
from jax.sharding import PartitionSpec as P

D = 256
COLS = 64
WIDE = D + 2 * COLS
PLANE = ("x", "v", "y")
ALL = ("y", "x", "w", "v", "c")
NY, NX, NW, NV, NC = 4, 4, 4, 2, 2
NP = NY * NX * NV
TILE_OWNER = 512
CHUNK = 512
SCALE_ROWS = 8
LANES = 128
SMALL = 4 * 2**20


def swap(v):
    return lax.ppermute(v, "c", [(0, 1), (1, 0)])


def shift(v, k):
    return lax.ppermute(v, "w", [(i, (i + k) % NW) for i in range(NW)])


def exchange(v):
    return lax.all_to_all(v, PLANE, 0, 0, tiled=True)


def pick(v, parts, start):
    rows = v.shape[0] // parts
    return lax.dynamic_slice(v, (start, 0), (rows, v.shape[1]), allow_negative_indices=False)


def repeat(v):
    return jnp.broadcast_to(v[None], (NP, *v.shape))


def along_w(v, root):
    away = (lax.axis_index("w") - root) % NW
    up, down, two = shift(v, 1), shift(v, -1), shift(v, 2)
    return jnp.where(away == 0, v, jnp.where(away == 1, up, jnp.where(away == 3, down, two)))


def all_w(v):
    return v, shift(v, 2), shift(v, 1), shift(v, -1)


def in_hbm(v):
    return pltpu.with_memory_space_constraint(v, pltpu.HBM)


def tie(*values):
    return lax.optimization_barrier(values)


def part_kernel(block_ref, part_ref, sem, *, mine):
    rows = part_ref.shape[0]
    core = lax.axis_index("c")
    first = pl.multiple_of((core if mine else 1 - core) * rows, rows)
    copy = pltpu.make_async_copy(block_ref.at[pl.ds(first, rows)], part_ref, sem)
    copy.start()
    copy.wait()


def part(block, mine):
    return pl.pallas_call(
        functools.partial(part_kernel, mine=mine),
        in_specs=[pl.BlockSpec(memory_space=pl.ANY)],
        out_specs=pl.BlockSpec(memory_space=pltpu.VMEM),
        out_shape=jax.ShapeDtypeStruct((block.shape[0] // NC, block.shape[1]), block.dtype),
        scratch_shapes=[pltpu.SemaphoreType.DMA],
        compiler_params=pltpu.CompilerParams(vmem_limit_bytes=SMALL),
    )(in_hbm(block))


def broadcast_half(block, owner):
    there, here = part(block, False), part(block, True)
    level = owner // NC % (NW * NV)
    chip = owner // (NC * NW * NV)
    at = {"y": (chip // NX, NY), "x": (chip % NX, NX), "v": (level % NV, NV)}
    start = 0
    for axis in PLANE:
        start = start * at[axis][1] + at[axis][0]
    start = start * (here.shape[0] // NP)
    here, other, level, start = tie(here, swap(there), level, start)
    half = jnp.where(owner % NC == lax.axis_index("c"), here, other)
    piece, late = tie(pick(exchange(half), NP, start), here)
    parts = (here, there, other, swap(late))
    piece = along_w(piece, level // NV)
    squares = jnp.concatenate([squared(part) for part in parts])[None, :]
    piece, squares, *parts = tie(piece, squares, *parts)
    return exchange(repeat(piece)).reshape(half.shape), parts, squares


def squared(block):
    wide = block[:, :D].astype(jnp.float32)
    return jnp.sum(wide * wide, axis=1) * (0.5 / D)


def scaling(top):
    power = jnp.floor(jnp.log2(jnp.maximum(jnp.max(top, axis=(0, 1), keepdims=True), 1e-30))) - 13.0
    return power, jnp.exp(power * -math.log(2.0))


def sum_pieces(v):
    groups = v.reshape(v.shape[0], -1, SCALE_ROWS, LANES).astype(jnp.float32)
    powers = groups[:, -1]
    piece = jnp.sum(groups[:, :-1] * jnp.exp2(powers)[:, None], axis=0)
    return jnp.concatenate([piece, jnp.max(powers, axis=0)[None]], axis=0).reshape(-1, LANES)


def join_kernel(*refs):
    parts, piece_ref, power_ref = refs[:-2], refs[-2], refs[-1]
    rows = parts[0].shape[0] - SCALE_ROWS
    piece = (parts[0][:rows] + parts[1][:rows]) + (parts[2][:rows] + parts[3][:rows])
    power = jnp.maximum(
        jnp.maximum(parts[0][rows:], parts[1][rows:]), jnp.maximum(parts[2][rows:], parts[3][rows:])
    ) + math.log2(NP * NW)
    factor = jnp.exp(power * -math.log(2.0))
    piece = (piece.reshape(-1, SCALE_ROWS, LANES) * factor[None]).reshape(rows, LANES)
    height = piece_ref.shape[0]
    for k in range(D // LANES):
        piece_ref[:, k * LANES : (k + 1) * LANES] = piece[k * height : (k + 1) * height]
        power_ref[:, k * LANES : (k + 1) * LANES] = power


def join(*parts):
    rows = (parts[0].shape[0] - SCALE_ROWS) * LANES // D
    return pl.pallas_call(
        join_kernel,
        out_shape=[
            jax.ShapeDtypeStruct((rows, D), jnp.float32),
            jax.ShapeDtypeStruct((SCALE_ROWS, D), jnp.float32),
        ],
        compiler_params=pltpu.CompilerParams(vmem_limit_bytes=SMALL),
    )(*parts)


def unscale(v, power, factor):
    groups = v.reshape(-1, SCALE_ROWS, D).astype(jnp.float32) * (jnp.exp2(power) * factor)
    return groups.reshape(-1, D)


def choose(step, refs):
    picked = refs[-1][...]
    for index in range(len(refs) - 1):
        picked = jnp.where(step == index, refs[index][...], picked)
    return picked


def mix_kernel(own_ref, a_ref, b_ref, c_ref, d_ref, sq_ref, mix_ref, term_ref, col_ref, total, own_sq, row_sum, *, steps):
    j = pl.program_id(0)
    rows = own_ref.shape[0]
    spans = [slice(i, i + TILE_OWNER) for i in range(0, rows, TILE_OWNER)]

    @pl.when(j == 0)
    def _():
        total[...] = jnp.zeros_like(total)
        row_sum[...] = jnp.zeros_like(row_sum)
        for span in spans:
            feat = own_ref[span, :D].astype(jnp.float32)
            own_sq[span, :] = jnp.sum(feat * feat, axis=1, keepdims=True) * (0.5 / D) + math.log(2.0 * math.sqrt(COLS))

    units = choose(j, (a_ref, b_ref, c_ref, d_ref))
    contract_last = (((1,), (1,)), ((), ()))
    chunks = [slice(i, i + CHUNK) for i in range(0, units.shape[0], CHUNK)]
    feats = [units[chunk, :D] for chunk in chunks]
    swapped = [jnp.concatenate([units[chunk, D + COLS :], units[chunk, D : D + COLS]], axis=1) for chunk in chunks]
    cols = [jnp.zeros((8, CHUNK), jnp.float32) for _ in chunks]
    for span in spans:
        lanes = row_sum[span, :]
        for k, chunk in enumerate(chunks):
            cross = lax.dot_general(own_ref[span, :D], feats[k], contract_last, preferred_element_type=jnp.float32)
            weight = lax.dot_general(own_ref[span, D:], swapped[k], contract_last, preferred_element_type=jnp.float32)
            mixed = weight * jnp.exp(cross * (1.0 / D) - sq_ref[:, chunk] - own_sq[span, :])
            mix_ref[span, chunk] = mixed.astype(jnp.bfloat16)
            cols[k] = cols[k] + jnp.sum(mixed.reshape(-1, 8, CHUNK), axis=0)
            for start in range(0, CHUNK, 128):
                lanes = lanes + mixed[:, start : start + 128]
        row_sum[span, :] = lanes
        total[span, :] += jnp.dot(mix_ref[span, :], units[:, :D], preferred_element_type=jnp.float32)
    for k, chunk in enumerate(chunks):
        col_ref[:, chunk] = cols[k]

    @pl.when(j == steps - 1)
    def _():
        top = jnp.zeros((8, D), jnp.float32)
        for span in spans:
            row_total = jnp.sum(row_sum[span, :], axis=1, keepdims=True)
            part = total[span, :] - row_total * own_ref[span, :D].astype(jnp.float32)
            total[span, :] = part
            top = jnp.maximum(top, jnp.max(jnp.abs(part).reshape(-1, 8, D), axis=0))
        power, factor = scaling(top)
        piece_rows = rows // NP
        for p in range(NP):
            scaled = total[p * piece_rows : (p + 1) * piece_rows, :] * factor
            for k in range(D // LANES):
                term_ref[p, k * piece_rows : (k + 1) * piece_rows] = scaled[:, k * LANES : (k + 1) * LANES]
            term_ref[p, D // LANES * piece_rows :] = jnp.broadcast_to(power, (SCALE_ROWS, LANES))


def mix(own, parts, unit_sq):
    rows, tile = own.shape[0], parts[0].shape[0]
    steps = len(parts)
    count = steps * tile
    packed_rows = D // LANES * rows // NP + SCALE_ROWS
    return pl.pallas_call(
        functools.partial(mix_kernel, steps=steps),
        grid=(steps,),
        in_specs=[pl.BlockSpec(memory_space=pltpu.VMEM)] * (1 + steps) + [pl.BlockSpec((1, tile), lambda j: (0, j))],
        out_specs=[
            pl.BlockSpec((rows, tile), lambda j: (0, j)),
            pl.BlockSpec((NP, packed_rows, LANES), lambda j: (0, 0, 0)),
            pl.BlockSpec((8, tile), lambda j: (0, j)),
        ],
        out_shape=[
            pltpu.HBM((rows, count), jnp.bfloat16),
            jax.ShapeDtypeStruct((NP, packed_rows, LANES), jnp.float32),
            jax.ShapeDtypeStruct((8, count), jnp.float32),
        ],
        scratch_shapes=[pltpu.VMEM((rows, D), jnp.float32), pltpu.VMEM((rows, 1), jnp.float32), pltpu.VMEM((rows, 128), jnp.float32)],
        compiler_params=pltpu.CompilerParams(
            vmem_limit_bytes=14 * 2**20, dimension_semantics=("arbitrary",)
        ),
        cost_estimate=pl.CostEstimate(
            flops=2 * rows * count * (WIDE + D),
            bytes_accessed=2 * rows * count + 2 * WIDE * (rows + count) + 4 * rows * D,
            transcendentals=rows * count,
        ),
    )(own, *parts, unit_sq)


def local_kernel(core_ref, mix_ref, own_ref, a_ref, b_ref, col_ref, *rest, scale):
    contract_first = (((0,), (0,)), ((), ()))
    out = lax.dot_general(mix_ref[...], own_ref[:, :D], contract_first, preferred_element_type=jnp.float32)
    total = jnp.sum(col_ref[...].T, axis=1, keepdims=True)
    units = choose(pl.program_id(0), (a_ref, b_ref))
    out = out - total * units[:, :D].astype(jnp.float32)
    if len(rest) == 2:
        out = (out + rest[0][...]) * scale
    rest[-1][...] = out


def local_terms(core, mixed, own, parts, col, first, received=None, scale=1.0):
    rows, tile = own.shape[0], parts[0].shape[0]
    count = len(parts) * tile
    whole = pl.BlockSpec(memory_space=pltpu.VMEM)
    ordered = pl.BlockSpec((tile, D), lambda j, core: (jnp.where(j == 0, core[0], 1 - core[0]), 0))
    more = [] if received is None else [received]
    return pl.pallas_call(
        functools.partial(local_kernel, scale=scale),
        grid_spec=pltpu.PrefetchScalarGridSpec(
            num_scalar_prefetch=1,
            grid=(len(parts),),
            in_specs=[
                pl.BlockSpec((rows, tile), lambda j, core: (0, j + first)),
                whole,
                whole,
                whole,
                pl.BlockSpec((8, tile), lambda j, core: (0, j + first)),
            ]
            + [ordered] * len(more),
            out_specs=ordered,
        ),
        out_shape=pltpu.HBM((count, D), jnp.float32),
        compiler_params=pltpu.CompilerParams(
            vmem_limit_bytes=14 * 2**20, dimension_semantics=("arbitrary",)
        ),
        cost_estimate=pl.CostEstimate(
            flops=2 * rows * count * D, bytes_accessed=2 * rows * count + 8 * count * D, transcendentals=0
        ),
    )(core, in_hbm(mixed), own, *parts, col, *more)


def place_kernel(half_ref, out_ref, sem):
    rows = half_ref.shape[0]
    first = pl.multiple_of(lax.axis_index("c") * rows, rows)
    copy = pltpu.make_async_copy(half_ref, out_ref.at[pl.ds(first, rows)], sem)
    copy.start()
    copy.wait()


def place(half):
    return pl.pallas_call(
        place_kernel,
        in_specs=[pl.BlockSpec(memory_space=pltpu.VMEM)],
        out_specs=pl.BlockSpec(memory_space=pl.ANY),
        out_shape=pltpu.HBM((NC * half.shape[0], half.shape[1]), half.dtype),
        scratch_shapes=[pltpu.SemaphoreType.DMA],
        compiler_params=pltpu.CompilerParams(vmem_limit_bytes=SMALL),
    )(half)


def local(unit_data, owner):
    rows = unit_data.shape[0]
    core = lax.axis_index("c").astype(jnp.int32).reshape(1)
    own, parts, squares = broadcast_half(unit_data, owner[0])
    mixed, term, col = mix(own, parts, squares)
    pieces = exchange(term.astype(jnp.float16))
    away = local_terms(core, mixed, own, parts[2:], col, 2)
    pieces, away = tie(pieces, away)
    received = swap(away)
    piece, power = join(*all_w(sum_pieces(pieces)))
    power_other = swap(power)
    mine = exchange(repeat(piece.astype(jnp.float16)))
    local_grad = local_terms(core, mixed, own, parts[:2], col, 0, received, 1.0 / math.sqrt(rows))
    mine, local_grad = tie(mine, local_grad)
    other = swap(mine)
    factor = 1.0 / math.sqrt(rows * NP * NW * NC)
    first = (1 - lax.axis_index("c")) * (rows // NC)
    owner_grad = lax.dynamic_update_slice(
        place(unscale(mine, power, factor)), unscale(other, power_other, factor), (first, 0), allow_negative_indices=False
    )
    return (owner_grad, local_grad)


def solution(mesh):
    grid = Mesh(np.asarray(mesh.devices).reshape(NY, NX, NW, NV, NC), ALL)
    in_specs = (P(ALL, None), P())
    out_specs = (P(), P(ALL, None))
    return jax.shard_map(local, mesh=grid, in_specs=in_specs, out_specs=out_specs, check_vma=False)
```
